512 devices in a mesh: leaf: 64 (over z, x), rows: 8 (over y, core).
Axes of the slice: x: 4, y: 4, z: 16, core: 2. Of those that a mesh axis runs over, the one named last changes fastest.
Arguments:
- right_side: bfloat16 [131072, 32], P(('leaf', 'rows')), may hold values from -6 to 6
- point_order: int32 [64, 2048], P('leaf'), may hold values from 0 to 2047, each once within a row
- leaf_inverse: bfloat16 [131072, 2048], P(('leaf', 'rows')), as said below
- bases: bfloat16 [131072, 6, 128], P(('leaf', 'rows'))
Outputs:
- solution: float32 [131072, 32], P(('leaf', 'rows'))
The draws below stay inside these ranges and needn't reach their ends.
Inputs may be any that keep to these rules, and one draw needn't show every extreme that they name: Each row of point_order names every index 0 .. 2047 once. Each leaf block of leaf_inverse is symmetric.
All inputs are finite; a program needn't handle non-finite values.
Results may differ from the reference program's by a relative error of at most 0.00045.
Values may be sent and summed in bfloat16 or wider, within the bound.
No kernel may reach another device: no remote copies, remote signals or barrier semaphores. Data moves between devices by JAX's collectives and lax.ppermute only.
A program may use at most 64 MiB of HBM per device.

```python
import jax
import jax.numpy as jnp
from jax import lax

LEAF = 2048
RANK = 128
NRHS = 32
LEVELS = 6
POINTS = 131072
N_LEAF = 64


def draw_leaf_inverse(key, part):
    key = jax.random.fold_in(key, 11)
    noise_key, diag_key = jax.random.split(key)
    raw = jax.random.normal(noise_key, (POINTS // LEAF, LEAF, LEAF), jnp.float32)
    noise = ((raw + jnp.swapaxes(raw, 1, 2)) * 0.5 ** 0.5).reshape(POINTS, LEAF)
    diagonal = jax.random.uniform(diag_key, (POINTS, 1), jnp.float32, 0.7, 1.3)
    position = jnp.arange(POINTS, dtype=jnp.int32)[:, None] % LEAF
    column = jnp.arange(LEAF, dtype=jnp.int32)[None, :]
    identity = (position == column).astype(jnp.float32)
    return (identity * diagonal + noise * (0.25 / LEAF ** 0.5)).astype(jnp.bfloat16)


def draw_bases(key, part):
    key = jax.random.fold_in(key, 23)
    raw = jax.random.normal(key, (POINTS, LEVELS, RANK), jnp.float32)
    height = jnp.arange(LEVELS).astype(jnp.float32)[None, :, None]
    scale = jnp.sqrt(0.5 / LEAF) * jnp.exp2(-0.5 * height)
    return (raw * scale).astype(jnp.bfloat16)


def shard_levels(rng, shape, cuts, smallest, high):
    loudness, own = 1.0, jax.random.fold_in(rng, 6)
    for axis_at, parts in cuts:
        steps = jnp.exp(jax.random.uniform(jax.random.fold_in(own, axis_at), (parts,), jnp.float32, smallest / len(cuts), high / len(cuts)))
        loudness = loudness * jnp.repeat(steps, shape[axis_at] // parts).reshape([-1 if axis == axis_at else 1 for axis in range(len(shape))])
    return loudness


def centred(own_key, shape, spread, bound, cuts=(), held_as=jnp.bfloat16):
    values = jax.random.normal(own_key, shape, jnp.float32) * spread
    if len(cuts) > 0:
        values = shard_levels(own_key, shape, cuts, -0.22, 0.18) * values
    return jnp.clip(values, min=-bound, max=bound).astype(held_as)


def setup_inputs(seed: int = 0) -> dict:
    splits = jax.random.split(jax.random.key(seed), 5)
    right_side = centred(splits[0], (POINTS, NRHS), 1.0, 6.0, ((0, 512),))
    point_order = jax.vmap(lambda own: jax.random.permutation(own, LEAF))(jax.random.split(splits[1], N_LEAF)).reshape((N_LEAF, LEAF)).astype(jnp.int32)
    leaf_inverse = draw_leaf_inverse(jax.random.fold_in(splits[4], 71), 0)
    bases = draw_bases(jax.random.fold_in(splits[4], 71), 0)
    return {"right_side": right_side, "point_order": point_order, "leaf_inverse": leaf_inverse, "bases": bases}


HIGHEST = lax.Precision.HIGHEST

def couple(own_a, own_p, far_a, far_p):
    extent = own_a.shape[-1]
    system = jnp.eye(extent, dtype=jnp.float32) - jnp.matmul(far_a, own_a, precision=HIGHEST)
    target = far_p - jnp.matmul(far_a, own_p, precision=HIGHEST)
    return jnp.linalg.solve(system, target)

def reference(right_side, point_order, leaf_inverse, bases):
    leaf_count, leaf_size = point_order.shape
    tiers = bases.shape[1]
    basis_width = bases.shape[2]
    total_points = leaf_count * leaf_size
    given = right_side.astype(jnp.float32).reshape(leaf_count, leaf_size, -1)
    ordered = jnp.take_along_axis(given, point_order.astype(jnp.int32)[:, :, None], axis=1)
    blocks = leaf_inverse.astype(jnp.float32).reshape(leaf_count, leaf_size, leaf_size)
    basis = bases.astype(jnp.float32)
    stacked = basis.reshape(leaf_count, leaf_size, tiers * basis_width)
    solved = jnp.einsum('bij,bjc->bic', blocks, ordered, precision=HIGHEST).reshape(total_points, -1)
    images = jnp.einsum('bij,bjc->bic', blocks, stacked, precision=HIGHEST).reshape(total_points, -1)
    rhs_width = solved.shape[1]
    widths = [images[:, k * basis_width:(k + 1) * basis_width] for k in range(tiers)]
    for height in range(tiers):
        span = leaf_size * 2 ** height
        live = jnp.concatenate([solved] + widths[height:], axis=1)
        columns = live.shape[1]
        groups = live.reshape(-1, span, columns)
        local_basis = basis[:, height, :].reshape(-1, span, basis_width)
        projected = jnp.einsum('gnk,gnc->gkc', local_basis, groups, precision=HIGHEST)
        projected = projected.reshape(-1, 2, basis_width, columns)
        own_a = projected[..., rhs_width:rhs_width + basis_width]
        own_p = jnp.concatenate([projected[..., :rhs_width], projected[..., rhs_width + basis_width:]], axis=-1)
        far_a = own_a[:, ::-1]
        far_p = own_p[:, ::-1]
        coeffs = couple(own_a, own_p, far_a, far_p).reshape(-1, basis_width, columns - basis_width)
        remain = jnp.concatenate([solved] + widths[height + 1:], axis=1).reshape(-1, span, columns - basis_width)
        current = widths[height].reshape(-1, span, basis_width)
        update = jnp.einsum('gnk,gkc->gnc', current, coeffs, precision=HIGHEST)
        remain = (remain - update).reshape(total_points, -1)
        solved = remain[:, :rhs_width]
        later = [remain[:, rhs_width + k * basis_width:rhs_width + (k + 1) * basis_width] for k in range(tiers - height - 1)]
        widths = widths[:height + 1] + later
    return solved
```

```python
import functools

import jax
import jax.numpy as jnp
from jax import lax
from jax.experimental import pallas as pl
from jax.experimental.pallas import tpu as pltpu
from jax.sharding import PartitionSpec as P

F32 = jnp.float32
BF16 = jnp.bfloat16
FULL = lax.Precision.HIGHEST
CORES = 2
VMEM_BYTES = 40 * 1024 * 1024


def mm(a, b, precision=FULL):
    return lax.dot_general(a, b, (((1,), (0,)), ((), ())), precision=precision, preferred_element_type=F32)


def mm_nt(a, b, precision=FULL):
    return lax.dot_general(a, b, (((1,), (1,)), ((), ())), precision=precision, preferred_element_type=F32)


def section_rows(height, tiers, rank, width):
    return width + rank * (tiers - height)


def section_offset(height, tiers, rank, width):
    return sum(section_rows(h, tiers, rank, width) for h in range(height))


def inverse_one_minus(left, right):
    rank = left.shape[0]
    eye = (
        lax.broadcasted_iota(jnp.int32, (rank, rank), 0) == lax.broadcasted_iota(jnp.int32, (rank, rank), 1)
    ).astype(F32)
    power = mm(left, right)
    system = eye - power
    guess = eye + power
    for _ in range(5):
        power = mm(power, power)
        guess = guess + mm(guess, power)

    def residual(x):
        gap = eye - mm(system, x)
        return gap, jnp.sum(gap * gap)

    gap, size = residual(guess)

    def restart():
        size_a = jnp.abs(system)
        bound = jnp.max(jnp.sum(size_a, axis=0)) * jnp.max(jnp.sum(size_a, axis=1))
        start = system.T / bound
        return (start,) + residual(start)

    def keep():
        return guess, gap, size

    def step(carry):
        count, x, gap, _ = carry
        x = x + mm(x, gap)
        return (count + 1, x) + residual(x)

    def more(carry):
        count, _, _, size = carry
        return jnp.logical_and(count < 80, jnp.logical_not(size < 1e-9))

    x, gap, size = lax.cond(size < 0.25, keep, restart)
    return lax.while_loop(more, step, (0, x, gap, size))[1]


def level_kernel(height, tiers, rank, width, own_ref, far_ref, *out_refs):
    rest = tiers - height - 1
    own = own_ref[0 : width + rank * (rest + 1), :]
    far = far_ref[0 : width + rank * (rest + 1), :]
    own_a, far_a = own[width : width + rank], far[width : width + rank]
    own_r, far_r = own[:width], far[:width]
    if rest > 0:
        own_r = jnp.concatenate([own_r, own[width + rank :]], axis=0)
        far_r = jnp.concatenate([far_r, far[width + rank :]], axis=0)
    target = far_r - mm(own_r, far_a)
    coeff = mm(target, inverse_one_minus(own_a, far_a))
    out_refs[0][...] = coeff
    if rest == 0:
        return
    other = own_r - mm(coeff, own_a)
    both = jnp.concatenate([coeff, other], axis=1)
    images = jnp.concatenate([own_r[width:], far_r[width:]], axis=1)
    base = width + rank * (rest + 1)
    top = mm_nt(both[:width], images)
    place = 0
    for g in range(rest):
        rows = width + rank * (rest - g)
        low = mm_nt(both[width + rank * g :], images[rank * g : rank * (g + 1)])
        part = jnp.concatenate([top[:, rank * g : rank * (g + 1)], low], axis=0)
        span = slice(base + place, base + place + rows)
        out_refs[1][place : place + rows, :] = own_ref[span, :] + far_ref[span, :] - part
        place += rows


def run_level(height, tiers, rank, width, own, far):
    rest = tiers - height - 1
    shapes = [jax.ShapeDtypeStruct((width + rank * rest, rank), F32)]
    left = own.shape[0] - section_rows(height, tiers, rank, width)
    if rest > 0:
        shapes.append(jax.ShapeDtypeStruct((left, rank), F32))
    return pl.pallas_call(
        functools.partial(level_kernel, height, tiers, rank, width),
        out_shape=shapes,
        in_specs=[pl.BlockSpec(memory_space=pltpu.VMEM)] * 2,
        out_specs=[pl.BlockSpec(memory_space=pltpu.VMEM)] * len(shapes),
        compiler_params=pltpu.CompilerParams(vmem_limit_bytes=VMEM_BYTES),
        name=f"level{height}",
    )(own, far)


def finish_kernel(tiers, rank, width, solved_ref, images_ref, *refs):
    coeff_refs, out_ref = refs[:tiers], refs[tiers]
    found = [None] * tiers
    for h in reversed(range(tiers)):
        value = coeff_refs[h][0:width, :]
        if h + 1 < tiers:
            above = jnp.concatenate(found[h + 1 :], axis=1)
            value = value - mm(above, coeff_refs[h][width:, :])
        found[h] = value
    out_ref[...] = solved_ref[...] - mm_nt(images_ref[...], jnp.concatenate(found, axis=1))


def finish(tiers, rank, width, solved, images, coeffs):
    return pl.pallas_call(
        functools.partial(finish_kernel, tiers, rank, width),
        out_shape=jax.ShapeDtypeStruct(solved.shape, F32),
        in_specs=[pl.BlockSpec(memory_space=pltpu.VMEM)] * (2 + tiers),
        out_specs=pl.BlockSpec(memory_space=pltpu.VMEM),
        compiler_params=pltpu.CompilerParams(vmem_limit_bytes=VMEM_BYTES),
        name="finish",
    )(solved, images, *coeffs)


def leaf_kernel(tiers, rank, width, inverse_ref, bases_ref, ordered_ref, own_ref, solved_ref, images_ref, gram_ref):
    inverse = inverse_ref[...]
    solved = mm(inverse, ordered_ref[...], None)
    images = mm(inverse, bases_ref[...], None)
    solved_ref[...] = solved
    images_ref[...] = images
    live = jnp.concatenate([images, solved], axis=1)
    high = live.astype(BF16)
    left = live - high.astype(F32)
    middle = left.astype(BF16)
    low = (left - middle.astype(F32)).astype(BF16)
    own = own_ref[...]

    def project(first, last, basis):
        total = None
        for piece in (high, middle, low):
            term = lax.dot_general(
                piece[:, first:last], basis, (((0,), (0,)), ((), ())), preferred_element_type=F32
            )
            total = term if total is None else total + term
        return total

    place = 0
    for h in range(tiers):
        basis = own[:, rank * h : rank * (h + 1)]
        gram_ref[place : place + width, :] = project(rank * tiers, rank * tiers + width, basis)
        rows = rank * (tiers - h)
        gram_ref[place + width : place + width + rows, :] = project(rank * h, rank * tiers, basis)
        place += width + rows


def leaf_step(tiers, rank, width, inverse, bases, ordered, own):
    rows = inverse.shape[0]
    total = section_offset(tiers, tiers, rank, width)
    return pl.pallas_call(
        functools.partial(leaf_kernel, tiers, rank, width),
        out_shape=[
            jax.ShapeDtypeStruct((rows, width), F32),
            jax.ShapeDtypeStruct((rows, tiers * rank), F32),
            jax.ShapeDtypeStruct((total, rank), F32),
        ],
        in_specs=[pl.BlockSpec(memory_space=pltpu.VMEM)] * 4,
        out_specs=[pl.BlockSpec(memory_space=pltpu.VMEM)] * 3,
        compiler_params=pltpu.CompilerParams(vmem_limit_bytes=VMEM_BYTES),
        name="leaf",
    )(inverse, bases, ordered, own)


def partner(value, axis, mask):
    return lax.ppermute(value, axis, [(i, i ^ mask) for i in range(lax.axis_size(axis))])


def local(right_side, point_order, leaf_inverse, bases):
    tiers, rank, width = bases.shape[1], bases.shape[2], right_side.shape[1]
    rows = bases.shape[0]
    flat = bases.reshape(rows, tiers * rank)
    given = lax.all_gather(right_side, "rows", axis=0, tiled=True)
    whole = lax.all_gather(flat, "rows", axis=0, tiled=True)
    ordered = jnp.take(given, point_order[0], axis=0, mode="clip")
    solved, images, gram = leaf_step(tiers, rank, width, leaf_inverse, whole, ordered, flat)

    members = lax.axis_size("rows")
    chips = members // CORES
    core = lax.axis_index("rows") % CORES
    groups = [[chip * CORES + c for chip in range(chips)] for c in range(CORES)]
    total = gram.shape[0]
    half = total // CORES
    keep = lax.dynamic_slice_in_dim(gram, core * half, half)
    give = lax.dynamic_slice_in_dim(gram, (1 - core) * half, half)
    keep = keep + partner(give, "rows", 1)
    parts = lax.all_to_all(keep.reshape(chips, half // chips, rank), "rows", 0, 0, axis_index_groups=groups)
    share = parts.sum(axis=0)
    spread = lax.all_to_all(
        jnp.broadcast_to(share[None], (chips, half // chips, rank)), "rows", 0, 0, axis_index_groups=groups
    )
    mine = spread.reshape(half, rank)

    def join(mine, theirs):
        first = jnp.where(core == 0, mine, theirs)
        second = jnp.where(core == 0, theirs, mine)
        return jnp.concatenate([first, second], axis=0)

    own = join(mine, partner(mine, "rows", 1))
    coeffs = []
    for height in range(tiers):
        if height < 2:
            half = own.shape[0] // CORES
            mine = lax.dynamic_slice_in_dim(own, core * half, half)
            got = partner(mine, "leaf", 2**height)
            far = join(got, partner(got, "rows", 1))
        else:
            far = partner(own, "leaf", 2**height)
        result = run_level(height, tiers, rank, width, own, far)
        coeffs.append(result[0])
        if height + 1 < tiers:
            own = result[1]
    return finish(tiers, rank, width, solved, images, coeffs)


def solution(mesh):
    in_specs = (
        P(("leaf", "rows"), None),
        P("leaf", None),
        P(("leaf", "rows"), None),
        P(("leaf", "rows"), None, None),
    )
    out_specs = P(("leaf", "rows"), None)
    return jax.shard_map(local, mesh=mesh, in_specs=in_specs, out_specs=out_specs, check_vma=False)
```

```python
import functools

import jax
import jax.numpy as jnp
from jax import lax
from jax.experimental import pallas as pl
from jax.experimental.pallas import tpu as pltpu
from jax.sharding import PartitionSpec as P

F32 = jnp.float32
BF16 = jnp.bfloat16
FULL = lax.Precision.HIGHEST
TRIPLE = lax.Precision.HIGH
DOUBLINGS = 3
MEMBERS = 8
CORES = 2
CHIPS = MEMBERS // CORES
PAD = 64
VMEM_BYTES = 16 * 1024 * 1024
BOTH = ("leaf", "rows")
NEAR = (1, 3, 4, 8, 16, 48)


def mm(a, b, precision=TRIPLE):
    return lax.dot_general(a, b, (((1,), (0,)), ((), ())), precision=precision, preferred_element_type=F32)


def mm_nt(a, b, precision=TRIPLE):
    return lax.dot_general(a, b, (((1,), (1,)), ((), ())), precision=precision, preferred_element_type=F32)


def share_rows(height, tiers, rank):
    return PAD // MEMBERS + (rank // MEMBERS) * (tiers - height)


def inverses(pairs):
    rank = pairs[0][0].shape[0]
    eye = (
        lax.broadcasted_iota(jnp.int32, (rank, rank), 0) == lax.broadcasted_iota(jnp.int32, (rank, rank), 1)
    ).astype(F32)
    powers = [mm(left, right) for left, right in pairs]
    systems = [eye - power for power in powers]
    guesses = [eye + power for power in powers]
    for _ in range(DOUBLINGS):
        powers = [mm(power, power) for power in powers]
        guesses = [guess + mm(guess, power) for guess, power in zip(guesses, powers)]
    gaps = [eye - mm(system, guess) for system, guess in zip(systems, guesses)]
    size = functools.reduce(jnp.maximum, [jnp.sum(gap * gap) for gap in gaps])

    def close():
        return [guess + mm(guess, gap) for guess, gap in zip(guesses, gaps)]

    def refine(left, right, guess):
        system = eye - mm(left, right, FULL)
        entries = jnp.abs(system)
        bound = jnp.max(jnp.sum(entries, axis=0)) * jnp.max(jnp.sum(entries, axis=1))

        def measured(x):
            gap = eye - mm(system, x, FULL)
            return x, gap, jnp.sum(gap * gap)

        def step(carry):
            count, _, x, gap, size = carry
            return (count + 1, size) + measured(x + mm(x, gap, FULL))

        def more(carry):
            count, before, _, _, size = carry
            falls = jnp.logical_and(size > 1e-10, size < 0.5 * before)
            return jnp.logical_and(count < 80, jnp.logical_or(size >= 0.25, falls))

        first = measured(guess)
        first = lax.cond(first[2] < 0.25, lambda: first, lambda: measured(system.T / bound))
        return lax.while_loop(more, step, (0, jnp.float32(jnp.inf)) + first)[2]

    def far_off():
        return [refine(left, right, guess) for (left, right), guess in zip(pairs, guesses)]

    return lax.cond(size < 1e-6, close, far_off)


def position(height):
    leaf, row = lax.axis_index("leaf"), lax.axis_index("rows")
    core = row % CORES
    return core, core * CHIPS + row // CORES, (leaf // 2**height) % 2


def without(section, width, rank):
    if section.shape[0] == width + rank:
        return section[:width]
    return jnp.concatenate([section[:width], section[width + rank :]], axis=0)


def couple(children, width, rank):
    blocks = [(s[width : width + rank], t[width : width + rank]) for s, t in children]
    found = []
    for (s, t), (s_a, t_a), inverse in zip(children, blocks, inverses(blocks)):
        s_r, t_r = without(s, width, rank), without(t, width, rank)
        s_c = mm(t_r - mm(s_r, t_a), inverse)
        found.append((s_c, s_r - mm(s_c, s_a)))
    return found


def images_of(s, t, width, rank):
    return jnp.concatenate([s[width + rank :], t[width + rank :]], axis=1)


def gathered(first, second, place, rank):
    low, each = PAD // MEMBERS, rank // MEMBERS

    def joined(start, rows):
        halves = [half[:, start : start + rows] for half in (first, second)]
        return jnp.concatenate([half.reshape(half.shape[0] * rows, rank) for half in halves], axis=0)

    def section(width, blocks):
        parts = [joined(place, low)[:width]]
        parts += [joined(place + low + each * k, each) for k in range(blocks)]
        return jnp.concatenate(parts, axis=0)

    return section


def share_level_kernel(height, tiers, rank, width, mine_ref, theirs_ref, coeff_ref, change_ref, wide_ref):
    rest = tiers - height - 1
    core, member, bit = position(height)
    mine, theirs = mine_ref[...], theirs_ref[...]
    first = jnp.where(core == 0, mine, theirs)
    second = jnp.where(core == 0, theirs, mine)
    s, t = [
        gathered(first[CHIPS * k : CHIPS * (k + 1)], second[CHIPS * k : CHIPS * (k + 1)], 0, rank)(width, rest + 1)
        for k in range(2)
    ]
    ((s_c, t_c),) = couple([(s, t)], width, rank)
    coeff_ref[...] = jnp.where(bit == 0, s_c, t_c)
    both = jnp.concatenate([s_c, t_c], axis=1)
    wide_ref[0:width, :] = both[:width]
    wide_ref[width:PAD, :] = jnp.zeros((PAD - width, 2 * rank), F32)
    wide_ref[PAD : PAD + rank * rest, :] = both[width:]
    low, each = PAD // MEMBERS, rank // MEMBERS
    slices = [wide_ref[pl.ds(pl.multiple_of(member * low, low), low), :]]
    for k in range(rest):
        slices.append(wide_ref[pl.ds(pl.multiple_of(PAD + rank * k + member * each, each), each), :])
    change = mm_nt(jnp.concatenate(slices, axis=0), images_of(s, t, width, rank))
    place = 0
    for g in range(rest):
        columns = slice(rank * g, rank * (g + 1))
        part = jnp.concatenate([change[:low, columns], change[low + each * g :, columns]], axis=0)
        rows = low + each * (rest - g)
        change_ref[place : place + rows, :] = part
        place += rows


def vmem(count):
    return [pl.BlockSpec(memory_space=pltpu.VMEM)] * count


def params():
    return pltpu.CompilerParams(vmem_limit_bytes=VMEM_BYTES)


def share_level(height, tiers, rank, width, mine, theirs):
    rest = tiers - height - 1
    rows = sum(share_rows(h, tiers, rank) for h in range(height + 1, tiers))
    return pl.pallas_call(
        functools.partial(share_level_kernel, height, tiers, rank, width),
        out_shape=[
            jax.ShapeDtypeStruct((width + rank * rest, rank), F32),
            jax.ShapeDtypeStruct((rows, rank), F32),
        ],
        in_specs=vmem(2),
        out_specs=vmem(2),
        scratch_shapes=[pltpu.VMEM((PAD + rank * rest, 2 * rank), F32)],
        compiler_params=params(),
        name=f"level{height}",
    )(mine, theirs)


def merged(coeffs, s, t, width, rank):
    both = jnp.concatenate(coeffs, axis=1)
    images = images_of(s[0], t[0], width, rank)
    top = mm_nt(both[:width], images)
    out = []
    for g in range(len(s) - 1):
        columns = slice(rank * g, rank * (g + 1))
        low = mm_nt(both[width + rank * g :], images[columns])
        out.append(s[g + 1] + t[g + 1] - jnp.concatenate([top[:, columns], low], axis=0))
    return out


def first_pair_kernel(height, tiers, rank, width, mine_ref, theirs_ref, coeff_ref, next_ref):
    core, _, bit = position(height)
    mine, theirs = mine_ref[...], theirs_ref[...]
    first = jnp.where(core == 0, mine, theirs)
    second = jnp.where(core == 0, theirs, mine)
    nodes = []
    for k in range(2):
        span = slice(CHIPS * k, CHIPS * (k + 1))
        place, sections = 0, []
        for h in range(height, tiers):
            sections.append(gathered(first[span], second[span], place, rank)(width, tiers - h))
            place += share_rows(h, tiers, rank)
        nodes.append(sections)
    join_pair(bit, nodes[0], nodes[1], width, rank, coeff_ref, next_ref)


def join_pair(bit, s, t, width, rank, coeff_ref, next_ref):
    (pair,) = couple([(s[0], t[0])], width, rank)
    coeff_ref[...] = jnp.where(bit == 0, pair[0], pair[1])
    place = 0
    for section in merged(pair, s, t, width, rank):
        next_ref[place : place + section.shape[0], :] = section
        place += section.shape[0]


def pair_kernel(height, tiers, rank, width, own_ref, got_ref, passed_ref, coeff_ref, next_ref):
    core, _, bit = position(height)
    own, got, passed = own_ref[...], got_ref[...], passed_ref[...]
    far = jnp.concatenate([jnp.where(core == 0, got, passed), jnp.where(core == 0, passed, got)], axis=0)
    lower = jnp.where(bit == 0, own, far)
    upper = jnp.where(bit == 0, far, own)

    def cut(value):
        place, out = 0, []
        for h in range(height, tiers):
            rows = width + rank * (tiers - h)
            out.append(value[place : place + rows])
            place += rows
        return out

    join_pair(bit, cut(lower), cut(upper), width, rank, coeff_ref, next_ref)


def pair_level(kernel, height, tiers, rank, width, *sections):
    rows = sum(width + rank * (tiers - h) for h in range(height + 1, tiers))
    return pl.pallas_call(
        functools.partial(kernel, height, tiers, rank, width),
        out_shape=[
            jax.ShapeDtypeStruct((width + rank * (tiers - height - 1), rank), F32),
            jax.ShapeDtypeStruct((rows, rank), F32),
        ],
        in_specs=vmem(len(sections)),
        out_specs=vmem(2),
        compiler_params=params(),
        name=f"level{height}",
    )(*sections)


def finish_kernel(tiers, rank, width, own_ref, far_ref, solved_ref, images_ref, *refs):
    coeff_refs, out_ref = refs[: tiers - 1], refs[tiers - 1]
    ((value, _),) = couple([(own_ref[...], far_ref[...])], width, rank)
    found = [None] * tiers
    found[tiers - 1] = value
    for h in reversed(range(tiers - 1)):
        above = jnp.concatenate(found[h + 1 :], axis=1)
        found[h] = coeff_refs[h][0:width, :] - mm(above, coeff_refs[h][width:, :])
    out_ref[...] = solved_ref[...] - mm_nt(images_ref[...], jnp.concatenate(found, axis=1))


def finish(tiers, rank, width, own, far, solved, images, coeffs):
    return pl.pallas_call(
        functools.partial(finish_kernel, tiers, rank, width),
        out_shape=jax.ShapeDtypeStruct(solved.shape, F32),
        in_specs=vmem(4 + len(coeffs)),
        out_specs=pl.BlockSpec(memory_space=pltpu.VMEM),
        compiler_params=params(),
        name="finish",
    )(own, far, solved, images, *coeffs)


def reorder_kernel(order_ref, inverse_ref, out_ref):
    columns = inverse_ref.shape[1]
    step = columns // MEMBERS
    inverse = inverse_ref[...]
    order = order_ref[...]
    for k in range(MEMBERS):
        given = lax.broadcasted_iota(jnp.int32, (step, columns), 0) + step * k
        chosen = jnp.where(given == order, 1.0, 0.0).astype(BF16)
        moved = lax.dot_general(inverse, chosen, (((1,), (1,)), ((), ())), preferred_element_type=F32)
        out_ref[:, step * k : step * (k + 1)] = moved.astype(BF16)


def reorder(order, inverse):
    return pl.pallas_call(
        reorder_kernel,
        out_shape=jax.ShapeDtypeStruct(inverse.shape, BF16),
        in_specs=vmem(2),
        out_specs=pl.BlockSpec(memory_space=pltpu.VMEM),
        compiler_params=params(),
        cost_estimate=pl.CostEstimate(
            flops=2 * inverse.size * inverse.shape[1], bytes_accessed=4 * inverse.size, transcendentals=0
        ),
        name="reorder",
    )(order, inverse)


def leaf_kernel(
    tiers, rank, width, inverse_ref, moved_ref, mine_ref, theirs_ref, own_ref, solved_ref, images_ref, gram_ref, images_vmem, sem
):
    rows = own_ref.shape[1]
    core = lax.axis_index("rows") % CORES
    images, solved = None, None
    for chip in range(CHIPS):
        for ref, side in ((mine_ref, core), (theirs_ref, 1 - core)):
            columns = pl.ds(pl.multiple_of((CORES * chip + side) * rows, rows), rows)
            wide = jnp.concatenate([ref[chip, h] for h in range(tiers)], axis=1)
            term = mm(inverse_ref[:, columns], wide, None)
            images = term if images is None else images + term
            term = mm(moved_ref[:, columns], ref[chip, tiers][:, :width], None)
            solved = term if solved is None else solved + term
    solved_ref[...] = solved
    images_vmem[...] = images
    copy = pltpu.make_async_copy(images_vmem, images_ref, sem)
    copy.start()
    live = jnp.concatenate([images, solved], axis=1)
    high = live.astype(BF16)
    left = live - high.astype(F32)
    middle = left.astype(BF16)
    low = (left - middle.astype(F32)).astype(BF16)

    def project(first, last, basis):
        total = None
        for piece in (high, middle, low):
            term = lax.dot_general(
                piece[:, first:last], basis, (((0,), (0,)), ((), ())), preferred_element_type=F32
            )
            total = term if total is None else total + term
        return total

    few, each = PAD // MEMBERS, rank // MEMBERS
    place = 0
    for h in range(tiers):
        basis = own_ref[h]
        top = project(rank * tiers, rank * tiers + width, basis)
        top = jnp.concatenate([top, jnp.zeros((PAD - width, rank), F32)], axis=0)
        gram_ref[:, place : place + few, :] = top.reshape(MEMBERS, few, rank)
        place += few
        body = project(rank * h, rank * tiers, basis)
        for k in range(tiers - h):
            block = body[rank * k : rank * (k + 1)]
            gram_ref[:, place : place + each, :] = block.reshape(MEMBERS, each, rank)
            place += each
    copy.wait()


def leaf_step(tiers, rank, width, inverse, moved, mine, theirs, own):
    rows = inverse.shape[0]
    share = sum(share_rows(h, tiers, rank) for h in range(tiers))
    return pl.pallas_call(
        functools.partial(leaf_kernel, tiers, rank, width),
        out_shape=[
            jax.ShapeDtypeStruct((rows, width), F32),
            jax.ShapeDtypeStruct((rows, tiers * rank), F32),
            jax.ShapeDtypeStruct((MEMBERS, share, rank), F32),
        ],
        in_specs=vmem(5),
        out_specs=vmem(1) + [pl.BlockSpec(memory_space=pl.ANY)] + vmem(1),
        scratch_shapes=[pltpu.VMEM((rows, tiers * rank), F32), pltpu.SemaphoreType.DMA],
        compiler_params=params(),
        name="leaf",
    )(inverse, moved, mine, theirs, own)


def swap_cores(value):
    return lax.ppermute(value, "rows", [(i, i ^ 1) for i in range(MEMBERS)])


def swap_leaves(value, mask):
    return lax.ppermute(value, "leaf", [(i, i ^ mask) for i in range(lax.axis_size("leaf"))])


def groups_of(sets):
    return [
        [leaf * MEMBERS + chip * CORES + core for leaf in leaves for chip in range(CHIPS)]
        for leaves in sets
        for core in range(CORES)
    ]


def spread(value, sets):
    groups = groups_of(sets)
    count = len(groups[0])
    return lax.all_to_all(
        jnp.broadcast_to(value[None], (count,) + value.shape), BOTH, 0, 0, axis_index_groups=groups
    )


def local(right_side, point_order, leaf_inverse, bases):
    tiers, rank, width = bases.shape[1], bases.shape[2], right_side.shape[1]
    leaves = range(lax.axis_size("leaf"))
    own = jnp.concatenate(
        [jnp.swapaxes(bases, 0, 1), jnp.pad(right_side, ((0, 0), (0, rank - width)))[None]], axis=0
    )
    groups = [[c + CORES * y for y in range(CHIPS)] for c in range(CORES)]
    mine = lax.all_to_all(jnp.broadcast_to(own[None], (CHIPS,) + own.shape), "rows", 0, 0, axis_index_groups=groups)
    theirs = swap_cores(mine)
    order, inverse, _ = lax.optimization_barrier((point_order, leaf_inverse, mine))
    moved = reorder(order, inverse)
    solved, images, gram = leaf_step(tiers, rank, width, leaf_inverse, moved, mine, theirs, own)

    core = lax.axis_index("rows") % CORES

    keep = lax.dynamic_slice_in_dim(gram, core * CHIPS, CHIPS)
    give = lax.dynamic_slice_in_dim(gram, (1 - core) * CHIPS, CHIPS)
    parts = keep + swap_cores(give)
    share = lax.all_to_all(parts, "rows", 0, 0, axis_index_groups=groups).sum(axis=0)

    coeffs = []
    for height in range(2):
        cut = share_rows(height, tiers, rank)
        section, own = share[:cut], share[cut:]
        far = swap_leaves(own, NEAR[height])
        sets = [(i, i ^ NEAR[height]) for i in leaves if not (i >> height) & 1]
        mine = spread(section, sets)
        theirs = swap_cores(mine)
        coeff, change = share_level(height, tiers, rank, width, mine, theirs)
        share = own + far - change
        coeffs.append(coeff)

    mine = spread(share, [(i, i ^ NEAR[2]) for i in leaves if not (i >> 2) & 1])
    theirs = swap_cores(mine)
    coeff, own = pair_level(first_pair_kernel, 2, tiers, rank, width, mine, theirs)
    coeffs.append(coeff)
    for height in range(3, tiers - 1):
        half = own.shape[0] // CORES
        got = swap_leaves(lax.dynamic_slice_in_dim(own, core * half, half), NEAR[height])
        passed = swap_cores(got)
        coeff, own = pair_level(pair_kernel, height, tiers, rank, width, own, got, passed)
        coeffs.append(coeff)
    far = swap_leaves(own, NEAR[5])
    return finish(tiers, rank, width, own, far, solved, images, coeffs)


def solution(mesh):
    in_specs = (
        P(("leaf", "rows"), None),
        P("leaf", None),
        P(("leaf", "rows"), None),
        P(("leaf", "rows"), None, None),
    )
    out_specs = P(("leaf", "rows"), None)
    return jax.shard_map(local, mesh=mesh, in_specs=in_specs, out_specs=out_specs, check_vma=False)
```

```python
import functools

import jax
import jax.numpy as jnp
from jax import lax
from jax.experimental import pallas as pl
from jax.experimental.pallas import tpu as pltpu
from jax.sharding import PartitionSpec as P

F32 = jnp.float32
BF16 = jnp.bfloat16
FULL = lax.Precision.HIGHEST
TRIPLE = lax.Precision.HIGH
DOUBLINGS = 3
MEMBERS = 8
CORES = 2
CHIPS = MEMBERS // CORES
PAD = 64
VMEM_BYTES = 16 * 1024 * 1024
BOTH = ("leaf", "rows")
NEAR = {2: 4, 3: 8, 4: 16, 5: 48}


def mm(a, b, precision=TRIPLE):
    return lax.dot_general(a, b, (((1,), (0,)), ((), ())), precision=precision, preferred_element_type=F32)


def mm_nt(a, b, precision=TRIPLE):
    return lax.dot_general(a, b, (((1,), (1,)), ((), ())), precision=precision, preferred_element_type=F32)


def share_rows(height, tiers, rank):
    return PAD // MEMBERS + (rank // MEMBERS) * (tiers - height)


def solve(pairs, targets):
    rank = pairs[0][0].shape[0]
    eye = (
        lax.broadcasted_iota(jnp.int32, (rank, rank), 0) == lax.broadcasted_iota(jnp.int32, (rank, rank), 1)
    ).astype(F32)
    powers = [mm(left, right) for left, right in pairs]
    systems = [eye - power for power in powers]
    guesses = [eye + power for power in powers]
    for _ in range(DOUBLINGS):
        powers = [mm(power, power) for power in powers]
        guesses = [guess + mm(guess, power) for guess, power in zip(guesses, powers)]
    gaps = [eye - mm(system, guess) for system, guess in zip(systems, guesses)]
    size = functools.reduce(jnp.maximum, [jnp.sum(gap * gap) for gap in gaps])

    firsts = [mm(target, guess) for target, guess in zip(targets, guesses)]

    def close():
        return [first + mm(first, gap) for first, gap in zip(firsts, gaps)]

    def refine(left, right, guess):
        system = eye - mm(left, right, FULL)
        entries = jnp.abs(system)
        bound = jnp.max(jnp.sum(entries, axis=0)) * jnp.max(jnp.sum(entries, axis=1))

        def measured(x):
            gap = eye - mm(system, x, FULL)
            return x, gap, jnp.sum(gap * gap)

        def step(carry):
            count, _, x, gap, size = carry
            return (count + 1, size) + measured(x + mm(x, gap, FULL))

        def more(carry):
            count, before, _, _, size = carry
            falls = jnp.logical_and(size > 1e-10, size < 0.5 * before)
            return jnp.logical_and(count < 80, jnp.logical_or(size >= 0.25, falls))

        first = measured(guess)
        first = lax.cond(first[2] < 0.25, lambda: first, lambda: measured(system.T / bound))
        return lax.while_loop(more, step, (0, jnp.float32(jnp.inf)) + first)[2]

    def far_off():
        found = [refine(left, right, guess) for (left, right), guess in zip(pairs, guesses)]
        return [mm(target, inverse, FULL) for target, inverse in zip(targets, found)]

    return lax.cond(size < 1e-6, close, far_off)


def position(height):
    leaf, row = lax.axis_index("leaf"), lax.axis_index("rows")
    core = row % CORES
    return core, core * CHIPS + row // CORES, (leaf // 2**height) % 2


def without(section, width, rank):
    if section.shape[0] == width + rank:
        return section[:width]
    return jnp.concatenate([section[:width], section[width + rank :]], axis=0)


def couple(children, width, rank):
    blocks = [(s[width : width + rank], t[width : width + rank]) for s, t in children]
    rests = [(without(s, width, rank), without(t, width, rank)) for s, t in children]
    targets = [t_r - mm(s_r, t_a) for (s_r, t_r), (_, t_a) in zip(rests, blocks)]
    found = solve(blocks, targets)
    return [(s_c, s_r - mm(s_c, s_a)) for s_c, (s_r, _), (s_a, _) in zip(found, rests, blocks)]


def images_of(s, t, width, rank):
    return jnp.concatenate([s[width + rank :], t[width + rank :]], axis=1)


def gathered(halves, node, place, rank):
    low, each = PAD // MEMBERS, rank // MEMBERS
    chips = slice(CHIPS * node, CHIPS * (node + 1))

    def joined(start, rows):
        return jnp.concatenate([half[chips, start : start + rows, :].reshape(CHIPS * rows, rank) for half in halves], axis=0)

    def section(width, blocks):
        parts = [joined(place, low)[:width]]
        parts += [joined(place + low + each * k, each) for k in range(blocks)]
        return jnp.concatenate(parts, axis=0)

    return section


def by_core(core, mine_ref, theirs_ref, body):
    @pl.when(core == 0)
    def _():
        body((mine_ref, theirs_ref))

    @pl.when(core != 0)
    def _():
        body((theirs_ref, mine_ref))


def vmem(count):
    return [pl.BlockSpec(memory_space=pltpu.VMEM)] * count


def params():
    return pltpu.CompilerParams(vmem_limit_bytes=VMEM_BYTES)


def own_rows(both, member, wide_ref, width, rank):
    rest = (both.shape[0] - width) // rank
    low, each = PAD // MEMBERS, rank // MEMBERS
    wide_ref[0:width, :] = both[:width]
    wide_ref[width:PAD, :] = jnp.zeros((PAD - width, 2 * rank), F32)
    wide_ref[PAD : PAD + rank * rest, :] = both[width:]
    slices = [wide_ref[pl.ds(pl.multiple_of(member * low, low), low), :]]
    for k in range(rest):
        slices.append(wide_ref[pl.ds(pl.multiple_of(PAD + rank * k + member * each, each), each), :])
    return jnp.concatenate(slices, axis=0)


def share_change(rows, images, skip, rank):
    low, each = PAD // MEMBERS, rank // MEMBERS
    parts = []
    for g in range(skip, images.shape[0] // rank):
        chosen = jnp.concatenate([rows[:low], rows[low + each * g :]], axis=0)
        parts.append(mm_nt(chosen, images[rank * g : rank * (g + 1)]))
    return jnp.concatenate(parts, axis=0)


def four_leaves_kernel(tiers, rank, width, mine_ref, theirs_ref, low_ref, high_ref, change_ref, *wide_refs):
    by_core(
        position(0)[0],
        mine_ref,
        theirs_ref,
        functools.partial(join_four, tiers, rank, width, low_ref, high_ref, change_ref, wide_refs),
    )


def join_four(tiers, rank, width, low_ref, high_ref, change_ref, wide_refs, halves):
    _, member, odd = position(0)
    upper = position(1)[2]
    place = share_rows(0, tiers, rank)
    nodes = [
        (gathered(halves, k, 0, rank)(width, tiers), gathered(halves, k, place, rank)(width, tiers - 1))
        for k in range(4)
    ]
    pairs = [(nodes[0], nodes[1]), (nodes[2], nodes[3])]
    found = couple([(s[0], t[0]) for s, t in pairs], width, rank)
    picked = [jnp.where(odd == 0, s_c, t_c) for s_c, t_c in found]
    low_ref[...] = jnp.where(upper == 0, picked[0], picked[1])
    change, joined = None, []
    for (s_c, t_c), (s, t), wide_ref in zip(found, pairs, wide_refs):
        both = jnp.concatenate([s_c, t_c], axis=1)
        images = images_of(s[0], t[0], width, rank)
        joined.append(s[1] + t[1] - mm_nt(both, images[:rank]))
        term = share_change(own_rows(both, member, wide_ref, width, rank), images, 1, rank)
        change = term if change is None else change + term
    ((s_c, t_c),) = couple([tuple(joined)], width, rank)
    high_ref[...] = jnp.where(upper == 0, s_c, t_c)
    both = jnp.concatenate([s_c, t_c], axis=1)
    rows = own_rows(both, member, wide_refs[2], width, rank)
    change_ref[...] = change + share_change(rows, images_of(*joined, width, rank), 0, rank)


def four_leaves(tiers, rank, width, mine, theirs):
    rows = sum(share_rows(h, tiers, rank) for h in range(2, tiers))
    return pl.pallas_call(
        functools.partial(four_leaves_kernel, tiers, rank, width),
        out_shape=[
            jax.ShapeDtypeStruct((width + rank * (tiers - 1), rank), F32),
            jax.ShapeDtypeStruct((width + rank * (tiers - 2), rank), F32),
            jax.ShapeDtypeStruct((rows, rank), F32),
        ],
        in_specs=vmem(2),
        out_specs=vmem(3),
        scratch_shapes=[pltpu.VMEM((PAD + rank * (tiers - k), 2 * rank), F32) for k in (1, 1, 2)],
        compiler_params=params(),
        name="level0",
    )(mine, theirs)


def merged(coeffs, s, t, width, rank):
    both = jnp.concatenate(coeffs, axis=1)
    images = images_of(s[0], t[0], width, rank)
    top = mm_nt(both[:width], images)
    out = []
    for g in range(len(s) - 1):
        columns = slice(rank * g, rank * (g + 1))
        low = mm_nt(both[width + rank * g :], images[columns])
        out.append(s[g + 1] + t[g + 1] - jnp.concatenate([top[:, columns], low], axis=0))
    return out


def first_pair_kernel(height, tiers, rank, width, mine_ref, theirs_ref, coeff_ref, next_ref):
    core, _, bit = position(height)

    def body(halves):
        nodes = []
        for k in range(2):
            place, sections = 0, []
            for h in range(height, tiers):
                sections.append(gathered(halves, k, place, rank)(width, tiers - h))
                place += share_rows(h, tiers, rank)
            nodes.append(sections)
        join_pair(bit, nodes[0], nodes[1], width, rank, coeff_ref, next_ref)

    by_core(core, mine_ref, theirs_ref, body)


def join_pair(bit, s, t, width, rank, coeff_ref, next_ref):
    (pair,) = couple([(s[0], t[0])], width, rank)
    coeff_ref[...] = jnp.where(bit == 0, pair[0], pair[1])
    place = 0
    for section in merged(pair, s, t, width, rank):
        next_ref[place : place + section.shape[0], :] = section
        place += section.shape[0]


def pair_kernel(height, tiers, rank, width, own_ref, got_ref, passed_ref, coeff_ref, next_ref):
    core, _, bit = position(height)
    own, got, passed = own_ref[...], got_ref[...], passed_ref[...]
    far = jnp.concatenate([jnp.where(core == 0, got, passed), jnp.where(core == 0, passed, got)], axis=0)
    lower = jnp.where(bit == 0, own, far)
    upper = jnp.where(bit == 0, far, own)

    def cut(value):
        place, out = 0, []
        for h in range(height, tiers):
            rows = width + rank * (tiers - h)
            out.append(value[place : place + rows])
            place += rows
        return out

    join_pair(bit, cut(lower), cut(upper), width, rank, coeff_ref, next_ref)


def pair_level(kernel, height, tiers, rank, width, *sections):
    rows = sum(width + rank * (tiers - h) for h in range(height + 1, tiers))
    return pl.pallas_call(
        functools.partial(kernel, height, tiers, rank, width),
        out_shape=[
            jax.ShapeDtypeStruct((width + rank * (tiers - height - 1), rank), F32),
            jax.ShapeDtypeStruct((rows, rank), F32),
        ],
        in_specs=vmem(len(sections)),
        out_specs=vmem(2),
        compiler_params=params(),
        name=f"level{height}",
    )(*sections)


def finish_kernel(tiers, rank, width, own_ref, far_ref, solved_ref, images_ref, *refs):
    coeff_refs, out_ref = refs[: tiers - 1], refs[tiers - 1]
    ((value, _),) = couple([(own_ref[...], far_ref[...])], width, rank)
    found = [None] * tiers
    found[tiers - 1] = value
    for h in reversed(range(tiers - 1)):
        above = jnp.concatenate(found[h + 1 :], axis=1)
        found[h] = coeff_refs[h][0:width, :] - mm(above, coeff_refs[h][width:, :])
    out_ref[...] = solved_ref[...] - mm_nt(images_ref[...], jnp.concatenate(found, axis=1)).T


def finish(tiers, rank, width, own, far, solved, images, coeffs):
    return pl.pallas_call(
        functools.partial(finish_kernel, tiers, rank, width),
        out_shape=jax.ShapeDtypeStruct(solved.shape, F32),
        in_specs=vmem(4 + len(coeffs)),
        out_specs=pl.BlockSpec(memory_space=pltpu.VMEM),
        compiler_params=params(),
        name="finish",
    )(own, far, solved, images, *coeffs)


def pack_kernel(bases_ref, given_ref, out_ref):
    tiers, rows, rank = bases_ref.shape
    width = given_ref.shape[0]
    for copy in range(CHIPS):
        for h in range(tiers):
            out_ref[copy, rows * h : rows * (h + 1), :] = bases_ref[h]
        for k in range(rows // rank):
            place = rows * tiers + width * k
            out_ref[copy, place : place + width, :] = given_ref[:, rank * k : rank * (k + 1)]


def pack(bases, given):
    tiers, rows, rank = bases.shape
    total = tiers * rows + given.size // rank
    return pl.pallas_call(
        pack_kernel,
        out_shape=jax.ShapeDtypeStruct((CHIPS, total, rank), bases.dtype),
        in_specs=vmem(2),
        out_specs=pl.BlockSpec(memory_space=pltpu.VMEM),
        compiler_params=params(),
        name="pack",
    )(bases, given)


def reorder_kernel(order_ref, inverse_ref, out_ref):
    columns = inverse_ref.shape[1]
    step = columns // MEMBERS
    inverse = inverse_ref[...]
    order = order_ref[...]
    for k in range(MEMBERS):
        given = lax.broadcasted_iota(jnp.int32, (step, columns), 0) + step * k
        chosen = jnp.where(given == order, 1.0, 0.0).astype(BF16)
        moved = lax.dot_general(inverse, chosen, (((1,), (1,)), ((), ())), preferred_element_type=F32)
        out_ref[:, step * k : step * (k + 1)] = moved.astype(BF16)


def reorder(order, inverse):
    return pl.pallas_call(
        reorder_kernel,
        out_shape=jax.ShapeDtypeStruct(inverse.shape, BF16),
        in_specs=vmem(2),
        out_specs=pl.BlockSpec(memory_space=pltpu.VMEM),
        compiler_params=params(),
        cost_estimate=pl.CostEstimate(
            flops=2 * inverse.size * inverse.shape[1], bytes_accessed=4 * inverse.size, transcendentals=0
        ),
        name="reorder",
    )(order, inverse)


def leaf_kernel(
    tiers, rank, width, inverse_ref, moved_ref, mine_ref, theirs_ref, own_ref, solved_ref, images_ref, keep_ref, give_ref, images_vmem, sem
):
    rows = inverse_ref.shape[0]
    core = lax.axis_index("rows") % CORES
    images, solved = None, None
    for chip in range(CHIPS):
        for ref, side in ((mine_ref, core), (theirs_ref, 1 - core)):
            columns = pl.ds(pl.multiple_of((CORES * chip + side) * rows, rows), rows)
            wide = jnp.concatenate([ref[chip, rows * h : rows * (h + 1)] for h in range(tiers)], axis=1)
            term = mm(inverse_ref[:, columns], wide, None)
            images = term if images is None else images + term
            given = ref[chip, rows * tiers :]
            given = jnp.concatenate([given[width * k : width * (k + 1)] for k in range(rows // rank)], axis=1)
            term = mm_nt(given, moved_ref[:, columns], None)
            solved = term if solved is None else solved + term
    solved_ref[...] = solved
    images_vmem[...] = images
    copy = pltpu.make_async_copy(images_vmem, images_ref, sem)
    copy.start()

    def pieces(value):
        high = value.astype(BF16)
        return high, (value - high.astype(F32)).astype(BF16)

    own = [own_ref[0, rows * h : rows * (h + 1)] for h in range(tiers)]
    flipped = jnp.concatenate(own, axis=1).T
    solved_high, solved_low = pieces(solved)
    few, each = PAD // MEMBERS, rank // MEMBERS

    def put(block, place, size):
        block = block.reshape(MEMBERS, size, rank)
        first, second = block[:CHIPS], block[CHIPS:]
        keep_ref[:, place : place + size, :] = jnp.where(core == 0, first, second)
        give_ref[:, place : place + size, :] = jnp.where(core == 0, second, first)

    place = 0
    for h in range(tiers):
        top = mm(solved_high, own[h], None) + mm(solved_low, own[h], None)
        put(jnp.concatenate([top, jnp.zeros((PAD - width, rank), F32)], axis=0), place, few)
        place += few
        high, low = pieces(images[:, rank * h : rank * (h + 1)])
        body = mm(flipped[rank * h :], high, None) + mm(flipped[rank * h :], low, None)
        for k in range(tiers - h):
            put(body[rank * k : rank * (k + 1)], place, each)
            place += each
    copy.wait()


def leaf_step(tiers, rank, width, inverse, moved, mine, theirs, own):
    rows = inverse.shape[0]
    share = sum(share_rows(h, tiers, rank) for h in range(tiers))
    return pl.pallas_call(
        functools.partial(leaf_kernel, tiers, rank, width),
        out_shape=[
            jax.ShapeDtypeStruct((width, rows), F32),
            jax.ShapeDtypeStruct((rows, tiers * rank), F32),
            jax.ShapeDtypeStruct((CHIPS, share, rank), F32),
            jax.ShapeDtypeStruct((CHIPS, share, rank), F32),
        ],
        in_specs=vmem(5),
        out_specs=vmem(1) + [pl.BlockSpec(memory_space=pl.ANY)] + vmem(2),
        scratch_shapes=[pltpu.VMEM((rows, tiers * rank), F32), pltpu.SemaphoreType.DMA],
        compiler_params=params(),
        name="leaf",
    )(inverse, moved, mine, theirs, own)


def swap_cores(value):
    return lax.ppermute(value, "rows", [(i, i ^ 1) for i in range(MEMBERS)])


def swap_leaves(value, mask):
    return lax.ppermute(value, "leaf", [(i, i ^ mask) for i in range(lax.axis_size("leaf"))])


def groups_of(sets):
    return [
        [leaf * MEMBERS + chip * CORES + core for leaf in leaves for chip in range(CHIPS)]
        for leaves in sets
        for core in range(CORES)
    ]


def spread(value, sets):
    groups = groups_of(sets)
    count = len(groups[0])
    return lax.all_to_all(
        jnp.broadcast_to(value[None], (count,) + value.shape), BOTH, 0, 0, axis_index_groups=groups
    )


def local(right_side, point_order, leaf_inverse, bases):
    tiers, rank, width = bases.shape[1], bases.shape[2], right_side.shape[1]
    leaves = range(lax.axis_size("leaf"))
    rows = bases.shape[0]
    packed = pack(jnp.swapaxes(bases, 0, 1), right_side.T)
    groups = [[c + CORES * y for y in range(CHIPS)] for c in range(CORES)]
    mine = lax.all_to_all(packed, "rows", 0, 0, axis_index_groups=groups)
    theirs = swap_cores(mine)
    order, inverse, _ = lax.optimization_barrier((point_order, leaf_inverse, mine))
    moved = reorder(order, inverse)
    solved, images, keep, give = leaf_step(tiers, rank, width, leaf_inverse, moved, mine, theirs, packed)

    parts = keep + swap_cores(give)
    share = lax.all_to_all(parts, "rows", 0, 0, axis_index_groups=groups).sum(axis=0)

    cut = share_rows(0, tiers, rank) + share_rows(1, tiers, rank)
    tail = share[cut:]
    mine = spread(share[:cut], [tuple(range(i, i + 4)) for i in leaves if i % 4 == 0])
    theirs = swap_cores(mine)
    tail = tail + swap_leaves(tail, 1)
    tail = tail + swap_leaves(tail, 3)
    low, high, change = four_leaves(tiers, rank, width, mine, theirs)
    share = tail - change
    coeffs = [low, high]

    mine = spread(share, [(i, i ^ NEAR[2]) for i in leaves if not (i >> 2) & 1])
    theirs = swap_cores(mine)
    coeff, own = pair_level(first_pair_kernel, 2, tiers, rank, width, mine, theirs)
    coeffs.append(coeff)
    core = lax.axis_index("rows") % CORES
    for height in range(3, tiers - 1):
        half = own.shape[0] // CORES
        got = swap_leaves(lax.dynamic_slice_in_dim(own, core * half, half), NEAR[height])
        passed = swap_cores(got)
        coeff, own = pair_level(pair_kernel, height, tiers, rank, width, own, got, passed)
        coeffs.append(coeff)
    far = swap_leaves(own, NEAR[5])
    return finish(tiers, rank, width, own, far, solved, images, coeffs).T


def solution(mesh):
    in_specs = (
        P(("leaf", "rows"), None),
        P("leaf", None),
        P(("leaf", "rows"), None),
        P(("leaf", "rows"), None, None),
    )
    out_specs = P(("leaf", "rows"), None)
    return jax.shard_map(local, mesh=mesh, in_specs=in_specs, out_specs=out_specs, check_vma=False)
```

```python
import functools

import jax
import jax.numpy as jnp
from jax import lax
from jax.experimental import pallas as pl
from jax.experimental.pallas import tpu as pltpu
from jax.sharding import PartitionSpec as P

F32 = jnp.float32
BF16 = jnp.bfloat16
FULL = lax.Precision.HIGHEST
TRIPLE = lax.Precision.HIGH
DOUBLINGS = 3
MEMBERS = 8
CORES = 2
CHIPS = MEMBERS // CORES
GRANULE = 8
VMEM_BYTES = 16 * 1024 * 1024
BOTH = ("leaf", "rows")
NEAR = {2: 4, 3: 8, 4: 16, 5: 48}


def mm(a, b, precision=TRIPLE):
    return lax.dot_general(a, b, (((1,), (0,)), ((), ())), precision=precision, preferred_element_type=F32)


def mm_nt(a, b, precision=TRIPLE):
    return lax.dot_general(a, b, (((1,), (1,)), ((), ())), precision=precision, preferred_element_type=F32)


def pair_rows(height, tiers, rank):
    return GRANULE + (rank // MEMBERS) * (2 * (tiers - height) - 1)


def places(height, first, tiers, rank):
    even = height - height % 2
    start = sum(pair_rows(h, tiers, rank) for h in range(first, even, 2))
    skipped = (rank // MEMBERS) * (tiers - even) if height % 2 else 0
    return start + (GRANULE // 2) * (height % 2), start + GRANULE + skipped


def solve(pairs, targets):
    rank = pairs[0][0].shape[0]
    eye = (
        lax.broadcasted_iota(jnp.int32, (rank, rank), 0) == lax.broadcasted_iota(jnp.int32, (rank, rank), 1)
    ).astype(F32)
    powers = [mm(left, right) for left, right in pairs]
    systems = [eye - power for power in powers]
    guesses = [eye + power for power in powers]
    for _ in range(DOUBLINGS):
        powers = [mm(power, power) for power in powers]
        guesses = [guess + mm(guess, power) for guess, power in zip(guesses, powers)]
    gaps = [eye - mm(system, guess) for system, guess in zip(systems, guesses)]
    size = functools.reduce(jnp.maximum, [jnp.sum(gap * gap) for gap in gaps])

    firsts = [mm(target, guess) for target, guess in zip(targets, guesses)]

    def close():
        return [first + mm(first, gap) for first, gap in zip(firsts, gaps)]

    def refine(left, right, guess):
        system = eye - mm(left, right, FULL)
        entries = jnp.abs(system)
        bound = jnp.max(jnp.sum(entries, axis=0)) * jnp.max(jnp.sum(entries, axis=1))

        def measured(x):
            gap = eye - mm(system, x, FULL)
            return x, gap, jnp.sum(gap * gap)

        def step(carry):
            count, _, x, gap, size = carry
            return (count + 1, size) + measured(x + mm(x, gap, FULL))

        def more(carry):
            count, before, _, _, size = carry
            falls = jnp.logical_and(size > 1e-10, size < 0.5 * before)
            return jnp.logical_and(count < 80, jnp.logical_or(size >= 0.25, falls))

        first = measured(guess)
        first = lax.cond(first[2] < 0.25, lambda: first, lambda: measured(system.T / bound))
        return lax.while_loop(more, step, (0, jnp.float32(jnp.inf)) + first)[2]

    def far_off():
        found = [refine(left, right, guess) for (left, right), guess in zip(pairs, guesses)]
        return [mm(target, inverse, FULL) for target, inverse in zip(targets, found)]

    return lax.cond(size < 1e-6, close, far_off)


def position(height):
    leaf, row = lax.axis_index("leaf"), lax.axis_index("rows")
    core = row % CORES
    return core, core * CHIPS + row // CORES, (leaf // 2**height) % 2


def without(section, width, rank):
    if section.shape[0] == width + rank:
        return section[:width]
    return jnp.concatenate([section[:width], section[width + rank :]], axis=0)


def couple(children, width, rank):
    blocks = [(s[width : width + rank], t[width : width + rank]) for s, t in children]
    rests = [(without(s, width, rank), without(t, width, rank)) for s, t in children]
    targets = [t_r - mm(s_r, t_a) for (s_r, t_r), (_, t_a) in zip(rests, blocks)]
    found = solve(blocks, targets)
    return [(s_c, s_r - mm(s_c, s_a)) for s_c, (s_r, _), (s_a, _) in zip(found, rests, blocks)]


def images_of(s, t, width, rank):
    return jnp.concatenate([s[width + rank :], t[width + rank :]], axis=1)


def gathered(halves, node, height, first, tiers, rank, width):
    each, few = rank // MEMBERS, width // MEMBERS
    chips = range(CHIPS * node, CHIPS * (node + 1))
    top, place = places(height, first, tiers, rank)
    parts = [half[chip, top : top + few, :] for half in halves for chip in chips]
    for k in range(tiers - height):
        rows = slice(place + each * k, place + each * (k + 1))
        parts += [half[chips.start : chips.stop, rows, :].reshape(CHIPS * each, rank) for half in halves]
    return jnp.concatenate(parts, axis=0)


def by_core(core, mine_ref, theirs_ref, body):
    @pl.when(core == 0)
    def _():
        body((mine_ref, theirs_ref))

    @pl.when(core != 0)
    def _():
        body((theirs_ref, mine_ref))


def vmem(count):
    return [pl.BlockSpec(memory_space=pltpu.VMEM)] * count


def params():
    return pltpu.CompilerParams(vmem_limit_bytes=VMEM_BYTES)


def own_rows(both, member, wide_ref, rank):
    each = rank // MEMBERS
    wide_ref[...] = both
    slices = [
        wide_ref[pl.ds(pl.multiple_of(rank * k + member * each, each), each), :] for k in range(both.shape[0] // rank)
    ]
    return jnp.concatenate(slices, axis=0)


def four_leaves_kernel(
    tiers, rank, width, mine_ref, theirs_ref, low_ref, high_ref, change_ref, wide_a, wide_b, wide_c, top_ref
):
    by_core(
        position(0)[0],
        mine_ref,
        theirs_ref,
        functools.partial(
            join_four, tiers, rank, width, low_ref, high_ref, change_ref, (wide_a, wide_b, wide_c), top_ref
        ),
    )


def join_four(tiers, rank, width, low_ref, high_ref, change_ref, wide_refs, top_ref, halves):
    _, member, odd = position(0)
    upper = position(1)[2]
    each, few = rank // MEMBERS, width // MEMBERS
    nodes = [[gathered(halves, k, h, 0, tiers, rank, width) for h in range(2)] for k in range(4)]
    tops, blocks = [None] * tiers, [None] * tiers

    def note(both, images, first, wide_ref):
        top = mm_nt(both[:width], images[rank * (2 - first) :])
        rows = own_rows(both[width:], member, wide_ref, rank)
        for h in range(2, tiers):
            g = h - first
            term = mm_nt(rows[each * g :], images[rank * g : rank * (g + 1)])
            part = top[:, rank * (h - 2) : rank * (h - 1)]
            blocks[h] = term if blocks[h] is None else blocks[h] + term
            tops[h] = part if tops[h] is None else tops[h] + part

    pairs = [(nodes[0], nodes[1]), (nodes[2], nodes[3])]
    found = couple([(s[0], t[0]) for s, t in pairs], width, rank)
    picked = [jnp.where(odd == 0, s_c, t_c) for s_c, t_c in found]
    low_ref[...] = jnp.where(upper == 0, picked[0], picked[1])
    joined = []
    for (s_c, t_c), (s, t), wide_ref in zip(found, pairs, wide_refs):
        both = jnp.concatenate([s_c, t_c], axis=1)
        images = images_of(s[0], t[0], width, rank)
        joined.append(s[1] + t[1] - mm_nt(both, images[:rank]))
        note(both, images, 1, wide_ref)
    ((s_c, t_c),) = couple([tuple(joined)], width, rank)
    high_ref[...] = jnp.where(upper == 0, s_c, t_c)
    note(jnp.concatenate([s_c, t_c], axis=1), images_of(*joined, width, rank), 2, wide_refs[2])
    for h in range(2, tiers):
        top, place = places(h, 2, tiers, rank)
        change_ref[place : place + each * (tiers - h), :] = blocks[h]
        for k in range(MEMBERS):
            top_ref[k, few * (h - 2) : few * (h - 1), :] = tops[h][few * k : few * (k + 1)]
    mine = top_ref[member]
    for h in range(2, tiers, 2):
        top, _ = places(h, 2, tiers, rank)
        change_ref[top : top + GRANULE, :] = mine[few * (h - 2) : few * h]


def four_leaves(tiers, rank, width, mine, theirs):
    rows = sum(pair_rows(h, tiers, rank) for h in range(2, tiers, 2))
    return pl.pallas_call(
        functools.partial(four_leaves_kernel, tiers, rank, width),
        out_shape=[
            jax.ShapeDtypeStruct((width + rank * (tiers - 1), rank), F32),
            jax.ShapeDtypeStruct((width + rank * (tiers - 2), rank), F32),
            jax.ShapeDtypeStruct((rows, rank), F32),
        ],
        in_specs=vmem(2),
        out_specs=vmem(3),
        scratch_shapes=[pltpu.VMEM((rank * (tiers - k), 2 * rank), F32) for k in (1, 1, 2)]
        + [pltpu.VMEM((MEMBERS, (width // MEMBERS) * (tiers - 2), rank), F32)],
        compiler_params=params(),
        name="level0",
    )(mine, theirs)


def merged(coeffs, s, t, width, rank):
    both = jnp.concatenate(coeffs, axis=1)
    images = images_of(s[0], t[0], width, rank)
    top = mm_nt(both[:width], images)
    out = []
    for g in range(len(s) - 1):
        columns = slice(rank * g, rank * (g + 1))
        low = mm_nt(both[width + rank * g :], images[columns])
        out.append(s[g + 1] + t[g + 1] - jnp.concatenate([top[:, columns], low], axis=0))
    return out


def first_pair_kernel(height, tiers, rank, width, mine_ref, theirs_ref, coeff_ref, next_ref):
    core, _, bit = position(height)

    def body(halves):
        nodes = [
            [gathered(halves, k, h, height, tiers, rank, width) for h in range(height, tiers)] for k in range(2)
        ]
        join_pair(bit, nodes[0], nodes[1], width, rank, coeff_ref, next_ref)

    by_core(core, mine_ref, theirs_ref, body)


def join_pair(bit, s, t, width, rank, coeff_ref, next_ref):
    (pair,) = couple([(s[0], t[0])], width, rank)
    coeff_ref[...] = jnp.where(bit == 0, pair[0], pair[1])
    place = 0
    for section in merged(pair, s, t, width, rank):
        next_ref[place : place + section.shape[0], :] = section
        place += section.shape[0]


def pair_kernel(height, tiers, rank, width, own_ref, got_ref, passed_ref, coeff_ref, next_ref):
    core, _, bit = position(height)
    own, got, passed = own_ref[...], got_ref[...], passed_ref[...]
    far = jnp.concatenate([jnp.where(core == 0, got, passed), jnp.where(core == 0, passed, got)], axis=0)
    lower = jnp.where(bit == 0, own, far)
    upper = jnp.where(bit == 0, far, own)

    def cut(value):
        place, out = 0, []
        for h in range(height, tiers):
            rows = width + rank * (tiers - h)
            out.append(value[place : place + rows])
            place += rows
        return out

    join_pair(bit, cut(lower), cut(upper), width, rank, coeff_ref, next_ref)


def pair_level(kernel, height, tiers, rank, width, *sections):
    rows = sum(width + rank * (tiers - h) for h in range(height + 1, tiers))
    return pl.pallas_call(
        functools.partial(kernel, height, tiers, rank, width),
        out_shape=[
            jax.ShapeDtypeStruct((width + rank * (tiers - height - 1), rank), F32),
            jax.ShapeDtypeStruct((rows, rank), F32),
        ],
        in_specs=vmem(len(sections)),
        out_specs=vmem(2),
        compiler_params=params(),
        name=f"level{height}",
    )(*sections)


def prepare_kernel(tiers, rank, width, solved_ref, images_ref, *refs):
    coeff_refs, out_ref = refs[:-1], refs[-1]
    last = tiers - 1
    found = [None] * last
    for h in reversed(range(last)):
        between = rank * (last - 1 - h)
        value = jnp.concatenate([coeff_refs[h][0:width, :], coeff_refs[h][width + between :, :]], axis=0)
        if between > 0:
            value = value - mm(jnp.concatenate(found[h + 1 :], axis=1), coeff_refs[h][width : width + between, :])
        found[h] = value
    images = images_ref[...]
    start = jnp.concatenate([solved_ref[...], images[:, rank * last :].T], axis=0)
    out_ref[...] = start - mm_nt(jnp.concatenate(found, axis=1), images[:, : rank * last])


def prepare(tiers, rank, width, solved, images, coeffs):
    rows = images.shape[0]
    return pl.pallas_call(
        functools.partial(prepare_kernel, tiers, rank, width),
        out_shape=jax.ShapeDtypeStruct((width + rank, rows), F32),
        in_specs=vmem(2 + len(coeffs)),
        out_specs=pl.BlockSpec(memory_space=pltpu.VMEM),
        compiler_params=params(),
        cost_estimate=pl.CostEstimate(
            flops=6 * (width + rank) * images.size, bytes_accessed=4 * images.size, transcendentals=0
        ),
        name="prepare",
    )(solved, images, *coeffs)


def finish_kernel(rank, width, own_ref, far_ref, ready_ref, out_ref):
    ((value, _),) = couple([(own_ref[...], far_ref[...])], width, rank)
    out_ref[...] = ready_ref[0:width, :] - mm(value, ready_ref[width:, :])


def finish(rank, width, own, far, ready):
    return pl.pallas_call(
        functools.partial(finish_kernel, rank, width),
        out_shape=jax.ShapeDtypeStruct((width, ready.shape[1]), F32),
        in_specs=vmem(3),
        out_specs=pl.BlockSpec(memory_space=pltpu.VMEM),
        compiler_params=params(),
        name="finish",
    )(own, far, ready)


def pack_kernel(bases_ref, given_ref, out_ref):
    tiers, rows, rank = bases_ref.shape
    width = given_ref.shape[0]
    for copy in range(CHIPS):
        for h in range(tiers):
            out_ref[copy, rows * h : rows * (h + 1), :] = bases_ref[h]
        for k in range(rows // rank):
            place = rows * tiers + width * k
            out_ref[copy, place : place + width, :] = given_ref[:, rank * k : rank * (k + 1)]


def pack(bases, given):
    tiers, rows, rank = bases.shape
    total = tiers * rows + given.size // rank
    return pl.pallas_call(
        pack_kernel,
        out_shape=jax.ShapeDtypeStruct((CHIPS, total, rank), bases.dtype),
        in_specs=vmem(2),
        out_specs=pl.BlockSpec(memory_space=pltpu.VMEM),
        compiler_params=params(),
        name="pack",
    )(bases, given)


def reorder_kernel(order_ref, inverse_ref, out_ref):
    columns = inverse_ref.shape[1]
    step = columns // MEMBERS
    inverse = inverse_ref[...]
    order = order_ref[...]
    for k in range(MEMBERS):
        given = lax.broadcasted_iota(jnp.int32, (step, columns), 0) + step * k
        chosen = jnp.where(given == order, 1.0, 0.0).astype(BF16)
        moved = lax.dot_general(inverse, chosen, (((1,), (1,)), ((), ())), preferred_element_type=F32)
        out_ref[:, step * k : step * (k + 1)] = moved.astype(BF16)


def reorder(order, inverse):
    return pl.pallas_call(
        reorder_kernel,
        out_shape=jax.ShapeDtypeStruct(inverse.shape, BF16),
        in_specs=vmem(2),
        out_specs=pl.BlockSpec(memory_space=pltpu.VMEM),
        compiler_params=params(),
        cost_estimate=pl.CostEstimate(
            flops=2 * inverse.size * inverse.shape[1], bytes_accessed=4 * inverse.size, transcendentals=0
        ),
        name="reorder",
    )(order, inverse)


def leaf_kernel(
    tiers, rank, width, inverse_ref, moved_ref, mine_ref, theirs_ref, own_ref, solved_ref, images_ref, keep_ref, give_ref, images_vmem, sem
):
    rows = inverse_ref.shape[0]
    core = lax.axis_index("rows") % CORES
    images, solved = None, None
    for chip in range(CHIPS):
        for ref, side in ((mine_ref, core), (theirs_ref, 1 - core)):
            columns = pl.ds(pl.multiple_of((CORES * chip + side) * rows, rows), rows)
            wide = jnp.concatenate([ref[chip, rows * h : rows * (h + 1)] for h in range(tiers)], axis=1)
            term = mm(inverse_ref[:, columns], wide, None)
            images = term if images is None else images + term
            given = ref[chip, rows * tiers :]
            given = jnp.concatenate([given[width * k : width * (k + 1)] for k in range(rows // rank)], axis=1)
            term = mm_nt(given, moved_ref[:, columns], None)
            solved = term if solved is None else solved + term
    solved_ref[...] = solved
    images_vmem[...] = images
    copy = pltpu.make_async_copy(images_vmem, images_ref, sem)
    copy.start()

    def pieces(value):
        high = value.astype(BF16)
        return high, (value - high.astype(F32)).astype(BF16)

    own = [own_ref[0, rows * h : rows * (h + 1)] for h in range(tiers)]
    flipped = jnp.concatenate(own, axis=1).T
    solved_high, solved_low = pieces(solved)
    few, each = width // MEMBERS, rank // MEMBERS

    def put(block, place, size):
        half = CHIPS * size
        first, second = block[:half], block[half:]
        for ref, value in (
            (keep_ref, jnp.where(core == 0, first, second)),
            (give_ref, jnp.where(core == 0, second, first)),
        ):
            if size % GRANULE == 0:
                ref[:, place : place + size, :] = value.reshape(CHIPS, size, rank)
                continue
            for chip in range(CHIPS):
                ref[chip, place : place + size, :] = value[size * chip : size * (chip + 1)]

    for h in range(tiers):
        top, place = places(h, 0, tiers, rank)
        put(mm(solved_high, own[h], None) + mm(solved_low, own[h], None), top, few)
        high, low = pieces(images[:, rank * h : rank * (h + 1)])
        body = mm(flipped[rank * h :], high, None) + mm(flipped[rank * h :], low, None)
        for k in range(tiers - h):
            put(body[rank * k : rank * (k + 1)], place + each * k, each)
    copy.wait()


def leaf_step(tiers, rank, width, inverse, moved, mine, theirs, own):
    rows = inverse.shape[0]
    share = sum(pair_rows(h, tiers, rank) for h in range(0, tiers, 2))
    return pl.pallas_call(
        functools.partial(leaf_kernel, tiers, rank, width),
        out_shape=[
            jax.ShapeDtypeStruct((width, rows), F32),
            jax.ShapeDtypeStruct((rows, tiers * rank), F32),
            jax.ShapeDtypeStruct((CHIPS, share, rank), F32),
            jax.ShapeDtypeStruct((CHIPS, share, rank), F32),
        ],
        in_specs=vmem(5),
        out_specs=vmem(1) + [pl.BlockSpec(memory_space=pl.ANY)] + vmem(2),
        scratch_shapes=[pltpu.VMEM((rows, tiers * rank), F32), pltpu.SemaphoreType.DMA],
        compiler_params=params(),
        name="leaf",
    )(inverse, moved, mine, theirs, own)


def swap_cores(value):
    return lax.ppermute(value, "rows", [(i, i ^ 1) for i in range(MEMBERS)])


def swap_leaves(value, mask):
    return lax.ppermute(value, "leaf", [(i, i ^ mask) for i in range(lax.axis_size("leaf"))])


def groups_of(sets):
    return [
        [leaf * MEMBERS + chip * CORES + core for leaf in leaves for chip in range(CHIPS)]
        for leaves in sets
        for core in range(CORES)
    ]


def spread(value, sets):
    groups = groups_of(sets)
    count = len(groups[0])
    return lax.all_to_all(
        jnp.broadcast_to(value[None], (count,) + value.shape), BOTH, 0, 0, axis_index_groups=groups
    )


def local(right_side, point_order, leaf_inverse, bases):
    tiers, rank, width = bases.shape[1], bases.shape[2], right_side.shape[1]
    leaves = range(lax.axis_size("leaf"))
    rows = bases.shape[0]
    packed = pack(jnp.swapaxes(bases, 0, 1), right_side.T)
    groups = [[c + CORES * y for y in range(CHIPS)] for c in range(CORES)]
    mine = lax.all_to_all(packed, "rows", 0, 0, axis_index_groups=groups)
    theirs = swap_cores(mine)
    order, inverse, _ = lax.optimization_barrier((point_order, leaf_inverse, mine))
    moved = reorder(order, inverse)
    solved, images, keep, give = leaf_step(tiers, rank, width, leaf_inverse, moved, mine, theirs, packed)

    parts = keep + swap_cores(give)
    share = lax.all_to_all(parts, "rows", 0, 0, axis_index_groups=groups).sum(axis=0)

    cut = pair_rows(0, tiers, rank)
    tail = share[cut:]
    mine = spread(share[:cut], [tuple(range(i, i + 4)) for i in leaves if i % 4 == 0])
    theirs = swap_cores(mine)
    tail = tail + swap_leaves(tail, 1)
    tail = tail + swap_leaves(tail, 3)
    low, high, change = four_leaves(tiers, rank, width, mine, theirs)
    share = tail - change
    coeffs = [low, high]

    mine = spread(share, [(i, i ^ NEAR[2]) for i in leaves if not (i >> 2) & 1])
    theirs = swap_cores(mine)
    coeff, own = pair_level(first_pair_kernel, 2, tiers, rank, width, mine, theirs)
    coeffs.append(coeff)
    core = lax.axis_index("rows") % CORES
    for height in range(3, tiers - 1):
        half = own.shape[0] // CORES
        got = swap_leaves(lax.dynamic_slice_in_dim(own, core * half, half), NEAR[height])
        passed = swap_cores(got)
        coeff, own = pair_level(pair_kernel, height, tiers, rank, width, own, got, passed)
        coeffs.append(coeff)
    far = swap_leaves(own, NEAR[5])
    ready = prepare(tiers, rank, width, solved, images, coeffs)
    return finish(rank, width, own, far, ready).T


def solution(mesh):
    in_specs = (
        P(("leaf", "rows"), None),
        P("leaf", None),
        P(("leaf", "rows"), None),
        P(("leaf", "rows"), None, None),
    )
    out_specs = P(("leaf", "rows"), None)
    return jax.shard_map(local, mesh=mesh, in_specs=in_specs, out_specs=out_specs, check_vma=False)
```

```python
import functools

import jax
import jax.numpy as jnp
from jax import lax
from jax.experimental import pallas as pl
from jax.experimental.pallas import tpu as pltpu
from jax.sharding import PartitionSpec as P

F32 = jnp.float32
BF16 = jnp.bfloat16
FULL = lax.Precision.HIGHEST
TRIPLE = lax.Precision.HIGH
DOUBLINGS = 3
MEMBERS = 8
CORES = 2
CHIPS = MEMBERS // CORES
GRANULE = 8
VMEM_BYTES = 16 * 1024 * 1024
BOTH = ("leaf", "rows")
NEAR = {2: 4, 3: 8, 4: 16, 5: 48}


def mm(a, b, precision=TRIPLE):
    return lax.dot_general(a, b, (((1,), (0,)), ((), ())), precision=precision, preferred_element_type=F32)


def mm_nt(a, b, precision=TRIPLE):
    return lax.dot_general(a, b, (((1,), (1,)), ((), ())), precision=precision, preferred_element_type=F32)


def pair_rows(height, tiers, rank):
    return GRANULE + (rank // MEMBERS) * (2 * (tiers - height) - 1)


def places(height, first, tiers, rank):
    even = height - height % 2
    start = sum(pair_rows(h, tiers, rank) for h in range(first, even, 2))
    skipped = (rank // MEMBERS) * (tiers - even) if height % 2 else 0
    return start + (GRANULE // 2) * (height % 2), start + GRANULE + skipped


def solve(pairs, targets):
    rank = pairs[0][0].shape[0]
    eye = (
        lax.broadcasted_iota(jnp.int32, (rank, rank), 0) == lax.broadcasted_iota(jnp.int32, (rank, rank), 1)
    ).astype(F32)
    powers = [mm(left, right) for left, right in pairs]
    systems = [eye - power for power in powers]
    guesses = [eye + power for power in powers]
    for _ in range(DOUBLINGS):
        powers = [mm(power, power) for power in powers]
        guesses = [guess + mm(guess, power) for guess, power in zip(guesses, powers)]
    gaps = [eye - mm(system, guess) for system, guess in zip(systems, guesses)]
    size = functools.reduce(jnp.maximum, [jnp.sum(gap * gap) for gap in gaps])

    firsts = [mm(target, guess) for target, guess in zip(targets, guesses)]

    def close():
        return [first + mm(first, gap) for first, gap in zip(firsts, gaps)]

    def refine(left, right, guess):
        system = eye - mm(left, right, FULL)
        entries = jnp.abs(system)
        bound = jnp.max(jnp.sum(entries, axis=0)) * jnp.max(jnp.sum(entries, axis=1))

        def measured(x):
            gap = eye - mm(system, x, FULL)
            return x, gap, jnp.sum(gap * gap)

        def step(carry):
            count, _, x, gap, size = carry
            return (count + 1, size) + measured(x + mm(x, gap, FULL))

        def more(carry):
            count, before, _, _, size = carry
            falls = jnp.logical_and(size > 1e-10, size < 0.5 * before)
            return jnp.logical_and(count < 80, jnp.logical_or(size >= 0.25, falls))

        first = measured(guess)
        first = lax.cond(first[2] < 0.25, lambda: first, lambda: measured(system.T / bound))
        return lax.while_loop(more, step, (0, jnp.float32(jnp.inf)) + first)[2]

    def far_off():
        found = [refine(left, right, guess) for (left, right), guess in zip(pairs, guesses)]
        return [mm(target, inverse, FULL) for target, inverse in zip(targets, found)]

    return lax.cond(size < 1e-6, close, far_off)


def position(height):
    leaf, row = lax.axis_index("leaf"), lax.axis_index("rows")
    core = row % CORES
    return core, core * CHIPS + row // CORES, (leaf // 2**height) % 2


def without(section, width, rank):
    if section.shape[0] == width + rank:
        return section[:width]
    return jnp.concatenate([section[:width], section[width + rank :]], axis=0)


def couple(children, width, rank):
    blocks = [(s[width : width + rank], t[width : width + rank]) for s, t in children]
    rests = [(without(s, width, rank), without(t, width, rank)) for s, t in children]
    targets = [t_r - mm(s_r, t_a) for (s_r, t_r), (_, t_a) in zip(rests, blocks)]
    found = solve(blocks, targets)
    return [(s_c, s_r - mm(s_c, s_a)) for s_c, (s_r, _), (s_a, _) in zip(found, rests, blocks)]


def images_of(s, t, width, rank):
    return jnp.concatenate([s[width + rank :], t[width + rank :]], axis=1)


def gathered(halves, node, height, first, tiers, rank, width):
    each, few = rank // MEMBERS, width // MEMBERS
    chips = range(CHIPS * node, CHIPS * (node + 1))
    top, place = places(height, first, tiers, rank)
    parts = [half[chip, top : top + few, :] for half in halves for chip in chips]
    for k in range(tiers - height):
        rows = slice(place + each * k, place + each * (k + 1))
        parts += [half[chips.start : chips.stop, rows, :].reshape(CHIPS * each, rank) for half in halves]
    return jnp.concatenate(parts, axis=0)


def by_core(core, mine_ref, theirs_ref, body):
    @pl.when(core == 0)
    def _():
        body((mine_ref, theirs_ref))

    @pl.when(core != 0)
    def _():
        body((theirs_ref, mine_ref))


def vmem(count):
    return [pl.BlockSpec(memory_space=pltpu.VMEM)] * count


def params():
    return pltpu.CompilerParams(vmem_limit_bytes=VMEM_BYTES)


def own_rows(both, member, wide_ref, rank):
    each = rank // MEMBERS
    wide_ref[...] = both
    slices = [
        wide_ref[pl.ds(pl.multiple_of(rank * k + member * each, each), each), :] for k in range(both.shape[0] // rank)
    ]
    return jnp.concatenate(slices, axis=0)


def four_leaves_kernel(
    tiers, rank, width, mine_ref, theirs_ref, low_ref, high_ref, change_ref, wide_a, wide_b, wide_c, top_ref
):
    by_core(
        position(0)[0],
        mine_ref,
        theirs_ref,
        functools.partial(
            join_four, tiers, rank, width, low_ref, high_ref, change_ref, (wide_a, wide_b, wide_c), top_ref
        ),
    )


def join_four(tiers, rank, width, low_ref, high_ref, change_ref, wide_refs, top_ref, halves):
    _, member, odd = position(0)
    upper = position(1)[2]
    each, few = rank // MEMBERS, width // MEMBERS
    nodes = [[gathered(halves, k, h, 0, tiers, rank, width) for h in range(2)] for k in range(4)]
    tops, blocks = [None] * tiers, [None] * tiers

    def note(both, images, first, wide_ref):
        top = mm_nt(both[:width], images[rank * (2 - first) :])
        rows = own_rows(both[width:], member, wide_ref, rank)
        for h in range(2, tiers):
            g = h - first
            term = mm_nt(rows[each * g :], images[rank * g : rank * (g + 1)])
            part = top[:, rank * (h - 2) : rank * (h - 1)]
            blocks[h] = term if blocks[h] is None else blocks[h] + term
            tops[h] = part if tops[h] is None else tops[h] + part

    pairs = [(nodes[0], nodes[1]), (nodes[2], nodes[3])]
    found = couple([(s[0], t[0]) for s, t in pairs], width, rank)
    picked = [jnp.where(odd == 0, s_c, t_c) for s_c, t_c in found]
    low_ref[...] = jnp.where(upper == 0, picked[0], picked[1])
    joined = []
    for (s_c, t_c), (s, t), wide_ref in zip(found, pairs, wide_refs):
        both = jnp.concatenate([s_c, t_c], axis=1)
        images = images_of(s[0], t[0], width, rank)
        joined.append(s[1] + t[1] - mm_nt(both, images[:rank]))
        note(both, images, 1, wide_ref)
    ((s_c, t_c),) = couple([tuple(joined)], width, rank)
    high_ref[...] = jnp.where(upper == 0, s_c, t_c)
    note(jnp.concatenate([s_c, t_c], axis=1), images_of(*joined, width, rank), 2, wide_refs[2])
    for h in range(2, tiers):
        top, place = places(h, 2, tiers, rank)
        change_ref[place : place + each * (tiers - h), :] = blocks[h]
        for k in range(MEMBERS):
            top_ref[k, few * (h - 2) : few * (h - 1), :] = tops[h][few * k : few * (k + 1)]
    mine = top_ref[member]
    for h in range(2, tiers, 2):
        top, _ = places(h, 2, tiers, rank)
        change_ref[top : top + GRANULE, :] = mine[few * (h - 2) : few * h]


def four_leaves(tiers, rank, width, mine, theirs):
    rows = sum(pair_rows(h, tiers, rank) for h in range(2, tiers, 2))
    return pl.pallas_call(
        functools.partial(four_leaves_kernel, tiers, rank, width),
        out_shape=[
            jax.ShapeDtypeStruct((width + rank * (tiers - 1), rank), F32),
            jax.ShapeDtypeStruct((width + rank * (tiers - 2), rank), F32),
            jax.ShapeDtypeStruct((rows, rank), F32),
        ],
        in_specs=vmem(2),
        out_specs=vmem(3),
        scratch_shapes=[pltpu.VMEM((rank * (tiers - k), 2 * rank), F32) for k in (1, 1, 2)]
        + [pltpu.VMEM((MEMBERS, (width // MEMBERS) * (tiers - 2), rank), F32)],
        compiler_params=params(),
        name="level0",
    )(mine, theirs)


def merged(coeffs, s, t, width, rank):
    both = jnp.concatenate(coeffs, axis=1)
    images = images_of(s[0], t[0], width, rank)
    top = mm_nt(both[:width], images)
    out = []
    for g in range(len(s) - 1):
        columns = slice(rank * g, rank * (g + 1))
        low = mm_nt(both[width + rank * g :], images[columns])
        out.append(s[g + 1] + t[g + 1] - jnp.concatenate([top[:, columns], low], axis=0))
    return out


def first_pair_kernel(height, tiers, rank, width, mine_ref, theirs_ref, coeff_ref, next_ref):
    core, _, bit = position(height)

    def body(halves):
        nodes = [
            [gathered(halves, k, h, height, tiers, rank, width) for h in range(height, tiers)] for k in range(2)
        ]
        join_pair(bit, nodes[0], nodes[1], width, rank, coeff_ref, next_ref)

    by_core(core, mine_ref, theirs_ref, body)


def mask_of(rank, compare):
    return compare(
        lax.broadcasted_iota(jnp.int32, (rank, rank), 0), lax.broadcasted_iota(jnp.int32, (rank, rank), 1)
    )


def fold_two(a, b):
    rank = a.shape[0]
    diagonal = jnp.sum(jnp.where(mask_of(rank, jnp.equal), b, 0.0), axis=0, keepdims=True)
    return jnp.concatenate(
        [jnp.where(mask_of(rank, jnp.greater_equal), a, b), jnp.broadcast_to(diagonal, (2 * GRANULE, rank))], axis=0
    )


def unfold_two(folded):
    rank = folded.shape[1]
    block = folded[:rank]
    flipped = block.T
    a = jnp.where(mask_of(rank, jnp.greater_equal), block, flipped)
    b = jnp.where(mask_of(rank, jnp.less), block, flipped)
    diagonal = jnp.broadcast_to(folded[rank : rank + 1], (rank, rank))
    return a, jnp.where(mask_of(rank, jnp.equal), diagonal, b)


def fold_one(a):
    half, part = a.shape[0] // 2, a.shape[0] // 4
    corner = a[half:, half:]
    return jnp.concatenate([a[:half], jnp.concatenate([corner[:part], corner[part:]], axis=1)], axis=0)


def unfold_one(folded):
    half = folded.shape[1] // 2
    upper, corner = folded[:half], folded[half:]
    corner = jnp.concatenate([corner[:, :half], corner[:, half:]], axis=0)
    return jnp.concatenate([upper, jnp.concatenate([upper.T[half:], corner], axis=1)], axis=0)


def folded_rows(height, tiers, rank, width):
    count = tiers - height
    pairs, single = count // 2, count % 2
    plain = sum(width + rank * (k - 1) for k in range(1, count + 1))
    return plain + pairs * (rank + 2 * GRANULE) + single * (3 * rank // 4)


def fold(sections, width, rank):
    parts = [without(section, width, rank) for section in sections]
    blocks = [section[width : width + rank] for section in sections]
    while len(blocks) > 1:
        parts.append(fold_two(blocks[0], blocks[1]))
        blocks = blocks[2:]
    parts += [fold_one(block) for block in blocks]
    return jnp.concatenate(parts, axis=0)


def unfold(value, height, tiers, rank, width):
    place, plain, blocks = 0, [], []
    for h in range(height, tiers):
        rows = width + rank * (tiers - h - 1)
        plain.append(value[place : place + rows])
        place += rows
    while len(blocks) + 1 < tiers - height:
        blocks += unfold_two(value[place : place + rank + 2 * GRANULE])
        place += rank + 2 * GRANULE
    if len(blocks) < tiers - height:
        blocks.append(unfold_one(value[place : place + 3 * rank // 4]))
    return [
        jnp.concatenate([part[:width], block] + ([part[width:]] if part.shape[0] > width else []), axis=0)
        for part, block in zip(plain, blocks)
    ]


def join_pair(bit, s, t, width, rank, coeff_ref, next_ref):
    (pair,) = couple([(s[0], t[0])], width, rank)
    coeff_ref[...] = jnp.where(bit == 0, pair[0], pair[1])
    next_ref[...] = fold(merged(pair, s, t, width, rank), width, rank)


def pair_kernel(height, tiers, rank, width, own_ref, got_ref, passed_ref, coeff_ref, next_ref):
    core, _, bit = position(height)
    own, got, passed = own_ref[...], got_ref[...], passed_ref[...]
    far = jnp.concatenate([jnp.where(core == 0, got, passed), jnp.where(core == 0, passed, got)], axis=0)
    lower = jnp.where(bit == 0, own, far)
    upper = jnp.where(bit == 0, far, own)
    s, t = [unfold(value, height, tiers, rank, width) for value in (lower, upper)]
    join_pair(bit, s, t, width, rank, coeff_ref, next_ref)


def pair_level(kernel, height, tiers, rank, width, *sections):
    rows = folded_rows(height + 1, tiers, rank, width)
    return pl.pallas_call(
        functools.partial(kernel, height, tiers, rank, width),
        out_shape=[
            jax.ShapeDtypeStruct((width + rank * (tiers - height - 1), rank), F32),
            jax.ShapeDtypeStruct((rows, rank), F32),
        ],
        in_specs=vmem(len(sections)),
        out_specs=vmem(2),
        compiler_params=params(),
        name=f"level{height}",
    )(*sections)


def prepare_kernel(tiers, rank, width, solved_ref, images_ref, *refs):
    coeff_refs, out_ref = refs[:-1], refs[-1]
    last = tiers - 1
    found = [None] * last
    for h in reversed(range(last)):
        between = rank * (last - 1 - h)
        value = jnp.concatenate([coeff_refs[h][0:width, :], coeff_refs[h][width + between :, :]], axis=0)
        if between > 0:
            value = value - mm(jnp.concatenate(found[h + 1 :], axis=1), coeff_refs[h][width : width + between, :])
        found[h] = value
    images = images_ref[...]
    start = jnp.concatenate([solved_ref[...], images[:, rank * last :].T], axis=0)
    out_ref[...] = start - mm_nt(jnp.concatenate(found, axis=1), images[:, : rank * last])


def prepare(tiers, rank, width, solved, images, coeffs):
    rows = images.shape[0]
    return pl.pallas_call(
        functools.partial(prepare_kernel, tiers, rank, width),
        out_shape=jax.ShapeDtypeStruct((width + rank, rows), F32),
        in_specs=vmem(2 + len(coeffs)),
        out_specs=pl.BlockSpec(memory_space=pltpu.VMEM),
        compiler_params=params(),
        cost_estimate=pl.CostEstimate(
            flops=6 * (width + rank) * images.size, bytes_accessed=4 * images.size, transcendentals=0
        ),
        name="prepare",
    )(solved, images, *coeffs)


def finish_kernel(rank, width, own_ref, far_ref, ready_ref, out_ref):
    (own,), (far,) = [unfold(ref[...], 0, 1, rank, width) for ref in (own_ref, far_ref)]
    ((value, _),) = couple([(own, far)], width, rank)
    out_ref[...] = ready_ref[0:width, :] - mm(value, ready_ref[width:, :])


def finish(rank, width, own, far, ready):
    return pl.pallas_call(
        functools.partial(finish_kernel, rank, width),
        out_shape=jax.ShapeDtypeStruct((width, ready.shape[1]), F32),
        in_specs=vmem(3),
        out_specs=pl.BlockSpec(memory_space=pltpu.VMEM),
        compiler_params=params(),
        name="finish",
    )(own, far, ready)


def pack_kernel(bases_ref, given_ref, out_ref):
    tiers, rows, rank = bases_ref.shape
    width = given_ref.shape[0]
    for copy in range(CHIPS):
        for h in range(tiers):
            out_ref[copy, rows * h : rows * (h + 1), :] = bases_ref[h]
        for k in range(rows // rank):
            place = rows * tiers + width * k
            out_ref[copy, place : place + width, :] = given_ref[:, rank * k : rank * (k + 1)]


def pack(bases, given):
    tiers, rows, rank = bases.shape
    total = tiers * rows + given.size // rank
    return pl.pallas_call(
        pack_kernel,
        out_shape=jax.ShapeDtypeStruct((CHIPS, total, rank), bases.dtype),
        in_specs=vmem(2),
        out_specs=pl.BlockSpec(memory_space=pltpu.VMEM),
        compiler_params=params(),
        name="pack",
    )(bases, given)


def reorder_kernel(order_ref, inverse_ref, out_ref):
    columns = inverse_ref.shape[1]
    step = columns // MEMBERS
    inverse = inverse_ref[...]
    order = order_ref[...]
    for k in range(MEMBERS):
        given = lax.broadcasted_iota(jnp.int32, (step, columns), 0) + step * k
        chosen = jnp.where(given == order, 1.0, 0.0).astype(BF16)
        moved = lax.dot_general(inverse, chosen, (((1,), (1,)), ((), ())), preferred_element_type=F32)
        out_ref[:, step * k : step * (k + 1)] = moved.astype(BF16)


def reorder(order, inverse):
    return pl.pallas_call(
        reorder_kernel,
        out_shape=jax.ShapeDtypeStruct(inverse.shape, BF16),
        in_specs=vmem(2),
        out_specs=pl.BlockSpec(memory_space=pltpu.VMEM),
        compiler_params=params(),
        cost_estimate=pl.CostEstimate(
            flops=2 * inverse.size * inverse.shape[1], bytes_accessed=4 * inverse.size, transcendentals=0
        ),
        name="reorder",
    )(order, inverse)


def leaf_kernel(
    tiers, rank, width, inverse_ref, moved_ref, mine_ref, theirs_ref, own_ref, solved_ref, images_ref, keep_ref, give_ref, images_vmem, sem
):
    rows = inverse_ref.shape[0]
    core = lax.axis_index("rows") % CORES
    images, solved = None, None
    for chip in range(CHIPS):
        for ref, side in ((mine_ref, core), (theirs_ref, 1 - core)):
            columns = pl.ds(pl.multiple_of((CORES * chip + side) * rows, rows), rows)
            wide = jnp.concatenate([ref[chip, rows * h : rows * (h + 1)] for h in range(tiers)], axis=1)
            term = mm(inverse_ref[:, columns], wide, None)
            images = term if images is None else images + term
            given = ref[chip, rows * tiers :]
            given = jnp.concatenate([given[width * k : width * (k + 1)] for k in range(rows // rank)], axis=1)
            term = mm_nt(given, moved_ref[:, columns], None)
            solved = term if solved is None else solved + term
    solved_ref[...] = solved
    images_vmem[...] = images
    copy = pltpu.make_async_copy(images_vmem, images_ref, sem)
    copy.start()

    def pieces(value):
        high = value.astype(BF16)
        return high, (value - high.astype(F32)).astype(BF16)

    own = [own_ref[0, rows * h : rows * (h + 1)] for h in range(tiers)]
    flipped = jnp.concatenate(own, axis=1).T
    solved_high, solved_low = pieces(solved)
    few, each = width // MEMBERS, rank // MEMBERS

    def put(block, place, size):
        half = CHIPS * size
        first, second = block[:half], block[half:]
        for ref, value in (
            (keep_ref, jnp.where(core == 0, first, second)),
            (give_ref, jnp.where(core == 0, second, first)),
        ):
            if size % GRANULE == 0:
                ref[:, place : place + size, :] = value.reshape(CHIPS, size, rank)
                continue
            for chip in range(CHIPS):
                ref[chip, place : place + size, :] = value[size * chip : size * (chip + 1)]

    for h in range(tiers):
        top, place = places(h, 0, tiers, rank)
        put(mm(solved_high, own[h], None) + mm(solved_low, own[h], None), top, few)
        high, low = pieces(images[:, rank * h : rank * (h + 1)])
        body = mm(flipped[rank * h :], high, None) + mm(flipped[rank * h :], low, None)
        for k in range(tiers - h):
            put(body[rank * k : rank * (k + 1)], place + each * k, each)
    copy.wait()


def leaf_step(tiers, rank, width, inverse, moved, mine, theirs, own):
    rows = inverse.shape[0]
    share = sum(pair_rows(h, tiers, rank) for h in range(0, tiers, 2))
    return pl.pallas_call(
        functools.partial(leaf_kernel, tiers, rank, width),
        out_shape=[
            jax.ShapeDtypeStruct((width, rows), F32),
            jax.ShapeDtypeStruct((rows, tiers * rank), F32),
            jax.ShapeDtypeStruct((CHIPS, share, rank), F32),
            jax.ShapeDtypeStruct((CHIPS, share, rank), F32),
        ],
        in_specs=vmem(5),
        out_specs=vmem(1) + [pl.BlockSpec(memory_space=pl.ANY)] + vmem(2),
        scratch_shapes=[pltpu.VMEM((rows, tiers * rank), F32), pltpu.SemaphoreType.DMA],
        compiler_params=params(),
        name="leaf",
    )(inverse, moved, mine, theirs, own)


def swap_cores(value):
    return lax.ppermute(value, "rows", [(i, i ^ 1) for i in range(MEMBERS)])


def swap_leaves(value, mask):
    return lax.ppermute(value, "leaf", [(i, i ^ mask) for i in range(lax.axis_size("leaf"))])


def groups_of(sets):
    return [
        [leaf * MEMBERS + chip * CORES + core for leaf in leaves for chip in range(CHIPS)]
        for leaves in sets
        for core in range(CORES)
    ]


def spread(value, sets):
    groups = groups_of(sets)
    count = len(groups[0])
    return lax.all_to_all(
        jnp.broadcast_to(value[None], (count,) + value.shape), BOTH, 0, 0, axis_index_groups=groups
    )


def local(right_side, point_order, leaf_inverse, bases):
    tiers, rank, width = bases.shape[1], bases.shape[2], right_side.shape[1]
    leaves = range(lax.axis_size("leaf"))
    rows = bases.shape[0]
    packed = pack(jnp.swapaxes(bases, 0, 1), right_side.T)
    groups = [[c + CORES * y for y in range(CHIPS)] for c in range(CORES)]
    mine = lax.all_to_all(packed, "rows", 0, 0, axis_index_groups=groups)
    theirs = swap_cores(mine)
    order, inverse, _ = lax.optimization_barrier((point_order, leaf_inverse, mine))
    moved = reorder(order, inverse)
    solved, images, keep, give = leaf_step(tiers, rank, width, leaf_inverse, moved, mine, theirs, packed)

    parts = keep + swap_cores(give)
    share = lax.all_to_all(parts, "rows", 0, 0, axis_index_groups=groups).sum(axis=0)

    cut = pair_rows(0, tiers, rank)
    tail = share[cut:]
    mine = spread(share[:cut], [tuple(range(i, i + 4)) for i in leaves if i % 4 == 0])
    theirs = swap_cores(mine)
    tail = tail + swap_leaves(tail, 1)
    tail = tail + swap_leaves(tail, 3)
    low, high, change = four_leaves(tiers, rank, width, mine, theirs)
    share = tail - change
    coeffs = [low, high]

    mine = spread(share, [(i, i ^ NEAR[2]) for i in leaves if not (i >> 2) & 1])
    theirs = swap_cores(mine)
    coeff, own = pair_level(first_pair_kernel, 2, tiers, rank, width, mine, theirs)
    coeffs.append(coeff)
    core = lax.axis_index("rows") % CORES
    for height in range(3, tiers - 1):
        half = own.shape[0] // CORES
        got = swap_leaves(lax.dynamic_slice_in_dim(own, core * half, half), NEAR[height])
        passed = swap_cores(got)
        coeff, own = pair_level(pair_kernel, height, tiers, rank, width, own, got, passed)
        coeffs.append(coeff)
    far = swap_leaves(own, NEAR[5])
    ready = prepare(tiers, rank, width, solved, images, coeffs)
    return finish(rank, width, own, far, ready).T


def solution(mesh):
    in_specs = (
        P(("leaf", "rows"), None),
        P("leaf", None),
        P(("leaf", "rows"), None),
        P(("leaf", "rows"), None, None),
    )
    out_specs = P(("leaf", "rows"), None)
    return jax.shard_map(local, mesh=mesh, in_specs=in_specs, out_specs=out_specs, check_vma=False)
```

```python
import functools

import jax
import jax.numpy as jnp
from jax import lax
from jax.experimental import pallas as pl
from jax.experimental.pallas import tpu as pltpu
from jax.sharding import PartitionSpec as P

F32 = jnp.float32
BF16 = jnp.bfloat16
FULL = lax.Precision.HIGHEST
TRIPLE = lax.Precision.HIGH
DOUBLINGS = 3
MEMBERS = 8
CORES = 2
CHIPS = MEMBERS // CORES
GRANULE = 8
VMEM_BYTES = 16 * 1024 * 1024
BOTH = ("leaf", "rows")
NEAR = {2: 4, 3: 8, 4: 16, 5: 48}


def mm(a, b, precision=TRIPLE):
    return lax.dot_general(a, b, (((1,), (0,)), ((), ())), precision=precision, preferred_element_type=F32)


def mm_nt(a, b, precision=TRIPLE):
    return lax.dot_general(a, b, (((1,), (1,)), ((), ())), precision=precision, preferred_element_type=F32)


def pair_rows(height, tiers, rank):
    return 2 * GRANULE + (rank // MEMBERS) * (2 * (tiers - height) - 2)


def places(height, first, tiers, rank):
    even = height - height % 2
    start = sum(pair_rows(h, tiers, rank) for h in range(first, even, 2))
    each = rank // MEMBERS
    skipped = each * (tiers - even - 1) if height % 2 else 0
    return start + (GRANULE // 2) * (height % 2), start + GRANULE, start + 2 * GRANULE + each + skipped


def solve(pairs, targets):
    rank = pairs[0][0].shape[0]
    eye = (
        lax.broadcasted_iota(jnp.int32, (rank, rank), 0) == lax.broadcasted_iota(jnp.int32, (rank, rank), 1)
    ).astype(F32)
    powers = [mm(left, right) for left, right in pairs]
    systems = [eye - power for power in powers]
    guesses = [eye + power for power in powers]
    for _ in range(DOUBLINGS):
        powers = [mm(power, power) for power in powers]
        guesses = [guess + mm(guess, power) for guess, power in zip(guesses, powers)]
    gaps = [eye - mm(system, guess) for system, guess in zip(systems, guesses)]
    size = functools.reduce(jnp.maximum, [jnp.sum(gap * gap) for gap in gaps])

    firsts = [mm(target, guess) for target, guess in zip(targets, guesses)]

    def close():
        return [first + mm(first, gap) for first, gap in zip(firsts, gaps)]

    def refine(left, right, guess):
        system = eye - mm(left, right, FULL)
        entries = jnp.abs(system)
        bound = jnp.max(jnp.sum(entries, axis=0)) * jnp.max(jnp.sum(entries, axis=1))

        def measured(x):
            gap = eye - mm(system, x, FULL)
            return x, gap, jnp.sum(gap * gap)

        def step(carry):
            count, _, x, gap, size = carry
            return (count + 1, size) + measured(x + mm(x, gap, FULL))

        def more(carry):
            count, before, _, _, size = carry
            falls = jnp.logical_and(size > 1e-10, size < 0.5 * before)
            return jnp.logical_and(count < 80, jnp.logical_or(size >= 0.25, falls))

        first = measured(guess)
        first = lax.cond(first[2] < 0.25, lambda: first, lambda: measured(system.T / bound))
        return lax.while_loop(more, step, (0, jnp.float32(jnp.inf)) + first)[2]

    def far_off():
        found = [refine(left, right, guess) for (left, right), guess in zip(pairs, guesses)]
        return [mm(target, inverse, FULL) for target, inverse in zip(targets, found)]

    return lax.cond(size < 1e-6, close, far_off)


def position(height):
    leaf, row = lax.axis_index("leaf"), lax.axis_index("rows")
    core = row % CORES
    return core, core * CHIPS + row // CORES, (leaf // 2**height) % 2


def without(section, width, rank):
    if section.shape[0] == width + rank:
        return section[:width]
    return jnp.concatenate([section[:width], section[width + rank :]], axis=0)


def couple(children, width, rank):
    blocks = [(s[width : width + rank], t[width : width + rank]) for s, t in children]
    rests = [(without(s, width, rank), without(t, width, rank)) for s, t in children]
    targets = [t_r - mm(s_r, t_a) for (s_r, t_r), (_, t_a) in zip(rests, blocks)]
    found = solve(blocks, targets)
    return [(s_c, s_r - mm(s_c, s_a)) for s_c, (s_r, _), (s_a, _) in zip(found, rests, blocks)]


def images_of(s, t, width, rank):
    return jnp.concatenate([s[width + rank :], t[width + rank :]], axis=1)


def gathered(halves, node, height, first, tiers, rank, width):
    each, few = rank // MEMBERS, width // MEMBERS
    chips = range(CHIPS * node, CHIPS * (node + 1))

    def joined(start):
        rows = slice(start, start + each)
        return [half[chips.start : chips.stop, rows, :].reshape(CHIPS * each, rank) for half in halves]

    _, middle, _ = places(height, first, tiers, rank)
    block = jnp.concatenate(joined(middle + GRANULE), axis=0)
    diagonal = sum(half[chip, middle : middle + 1, :] for half in halves for chip in chips)
    blocks = unfold_two(jnp.concatenate([block, diagonal], axis=0))
    sections = []
    for h in (height, height + 1):
        top, _, place = places(h, first, tiers, rank)
        parts = [half[chip, top : top + few, :] for half in halves for chip in chips] + [blocks[h - height]]
        for k in range(tiers - h - 1):
            parts += joined(place + each * k)
        sections.append(jnp.concatenate(parts, axis=0))
    return sections


def by_core(core, mine_ref, theirs_ref, body):
    @pl.when(core == 0)
    def _():
        body((mine_ref, theirs_ref))

    @pl.when(core != 0)
    def _():
        body((theirs_ref, mine_ref))


def vmem(count):
    return [pl.BlockSpec(memory_space=pltpu.VMEM)] * count


def params():
    return pltpu.CompilerParams(vmem_limit_bytes=VMEM_BYTES)


def own_rows(both, member, wide_ref, rank):
    each = rank // MEMBERS
    wide_ref[...] = both
    slices = [
        wide_ref[pl.ds(pl.multiple_of(rank * k + member * each, each), each), :] for k in range(both.shape[0] // rank)
    ]
    return jnp.concatenate(slices, axis=0)


def four_leaves_kernel(
    tiers, rank, width, mine_ref, theirs_ref, low_ref, high_ref, change_ref, wide_a, wide_b, wide_c, top_ref
):
    by_core(
        position(0)[0],
        mine_ref,
        theirs_ref,
        functools.partial(
            join_four, tiers, rank, width, low_ref, high_ref, change_ref, (wide_a, wide_b, wide_c), top_ref
        ),
    )


def join_four(tiers, rank, width, low_ref, high_ref, change_ref, wide_refs, top_ref, halves):
    _, member, odd = position(0)
    upper = position(1)[2]
    each, few = rank // MEMBERS, width // MEMBERS
    nodes = [gathered(halves, k, 0, 0, tiers, rank, width) for k in range(4)]
    tops, blocks = [None] * tiers, [None] * tiers

    def note(both, images, first, wide_ref):
        top = mm_nt(both[:width], images[rank * (2 - first) :])
        rows = own_rows(both[width:], member, wide_ref, rank)
        for h in range(2, tiers):
            g = h - first
            term = mm_nt(rows[each * g :], images[rank * g : rank * (g + 1)])
            part = top[:, rank * (h - 2) : rank * (h - 1)]
            blocks[h] = term if blocks[h] is None else blocks[h] + term
            tops[h] = part if tops[h] is None else tops[h] + part

    pairs = [(nodes[0], nodes[1]), (nodes[2], nodes[3])]
    found = couple([(s[0], t[0]) for s, t in pairs], width, rank)
    picked = [jnp.where(odd == 0, s_c, t_c) for s_c, t_c in found]
    low_ref[...] = jnp.where(upper == 0, picked[0], picked[1])
    joined = []
    for (s_c, t_c), (s, t), wide_ref in zip(found, pairs, wide_refs):
        both = jnp.concatenate([s_c, t_c], axis=1)
        images = images_of(s[0], t[0], width, rank)
        joined.append(s[1] + t[1] - mm_nt(both, images[:rank]))
        note(both, images, 1, wide_ref)
    ((s_c, t_c),) = couple([tuple(joined)], width, rank)
    high_ref[...] = jnp.where(upper == 0, s_c, t_c)
    note(jnp.concatenate([s_c, t_c], axis=1), images_of(*joined, width, rank), 2, wide_refs[2])
    for h in range(2, tiers):
        _, _, place = places(h, 2, tiers, rank)
        if h + 1 < tiers:
            change_ref[place : place + each * (tiers - h - 1), :] = blocks[h][each:]
        for k in range(MEMBERS):
            top_ref[k, few * (h - 2) : few * (h - 1), :] = tops[h][few * k : few * (k + 1)]
    mine = top_ref[member]
    row = lax.broadcasted_iota(jnp.int32, (each, rank), 0) + member * each
    column = lax.broadcasted_iota(jnp.int32, (each, rank), 1)
    for h in range(2, tiers, 2):
        top, middle, _ = places(h, 2, tiers, rank)
        change_ref[top : top + GRANULE, :] = mine[few * (h - 2) : few * h]
        a, b = blocks[h][:each], blocks[h + 1][:each]
        diagonal = jnp.sum(jnp.where(row == column, b, 0.0), axis=0, keepdims=True)
        change_ref[middle : middle + GRANULE, :] = jnp.broadcast_to(diagonal, (GRANULE, rank))
        change_ref[middle + GRANULE : middle + GRANULE + each, :] = jnp.where(row >= column, a, b)


def four_leaves(tiers, rank, width, mine, theirs):
    rows = sum(pair_rows(h, tiers, rank) for h in range(2, tiers, 2))
    return pl.pallas_call(
        functools.partial(four_leaves_kernel, tiers, rank, width),
        out_shape=[
            jax.ShapeDtypeStruct((width + rank * (tiers - 1), rank), F32),
            jax.ShapeDtypeStruct((width + rank * (tiers - 2), rank), F32),
            jax.ShapeDtypeStruct((rows, rank), F32),
        ],
        in_specs=vmem(2),
        out_specs=vmem(3),
        scratch_shapes=[pltpu.VMEM((rank * (tiers - k), 2 * rank), F32) for k in (1, 1, 2)]
        + [pltpu.VMEM((MEMBERS, (width // MEMBERS) * (tiers - 2), rank), F32)],
        compiler_params=params(),
        name="level0",
    )(mine, theirs)


def merged(coeffs, s, t, width, rank):
    both = jnp.concatenate(coeffs, axis=1)
    images = images_of(s[0], t[0], width, rank)
    top = mm_nt(both[:width], images)
    out = []
    for g in range(len(s) - 1):
        columns = slice(rank * g, rank * (g + 1))
        low = mm_nt(both[width + rank * g :], images[columns])
        out.append(s[g + 1] + t[g + 1] - jnp.concatenate([top[:, columns], low], axis=0))
    return out


def first_pair_kernel(height, tiers, rank, width, mine_ref, theirs_ref, coeff_ref, next_ref):
    core, _, bit = position(height)

    def body(halves):
        nodes = [
            sum([gathered(halves, k, h, height, tiers, rank, width) for h in range(height, tiers, 2)], []) for k in range(2)
        ]
        join_pair(bit, nodes[0], nodes[1], width, rank, coeff_ref, next_ref)

    by_core(core, mine_ref, theirs_ref, body)


def mask_of(rank, compare):
    return compare(
        lax.broadcasted_iota(jnp.int32, (rank, rank), 0), lax.broadcasted_iota(jnp.int32, (rank, rank), 1)
    )


def fold_two(a, b):
    rank = a.shape[0]
    diagonal = jnp.sum(jnp.where(mask_of(rank, jnp.equal), b, 0.0), axis=0, keepdims=True)
    return jnp.concatenate(
        [jnp.where(mask_of(rank, jnp.greater_equal), a, b), jnp.broadcast_to(diagonal, (2 * GRANULE, rank))], axis=0
    )


def unfold_two(folded):
    rank = folded.shape[1]
    block = folded[:rank]
    flipped = block.T
    a = jnp.where(mask_of(rank, jnp.greater_equal), block, flipped)
    b = jnp.where(mask_of(rank, jnp.less), block, flipped)
    diagonal = jnp.broadcast_to(folded[rank : rank + 1], (rank, rank))
    return a, jnp.where(mask_of(rank, jnp.equal), diagonal, b)


def fold_one(a):
    half, part = a.shape[0] // 2, a.shape[0] // 4
    corner = a[half:, half:]
    return jnp.concatenate([a[:half], jnp.concatenate([corner[:part], corner[part:]], axis=1)], axis=0)


def unfold_one(folded):
    half = folded.shape[1] // 2
    upper, corner = folded[:half], folded[half:]
    corner = jnp.concatenate([corner[:, :half], corner[:, half:]], axis=0)
    return jnp.concatenate([upper, jnp.concatenate([upper.T[half:], corner], axis=1)], axis=0)


def folded_rows(height, tiers, rank, width):
    count = tiers - height
    pairs, single = count // 2, count % 2
    plain = sum(width + rank * (k - 1) for k in range(1, count + 1))
    return plain + pairs * (rank + 2 * GRANULE) + single * (3 * rank // 4)


def fold(sections, width, rank):
    parts = [without(section, width, rank) for section in sections]
    blocks = [section[width : width + rank] for section in sections]
    while len(blocks) > 1:
        parts.append(fold_two(blocks[0], blocks[1]))
        blocks = blocks[2:]
    parts += [fold_one(block) for block in blocks]
    return jnp.concatenate(parts, axis=0)


def unfold(value, height, tiers, rank, width):
    place, plain, blocks = 0, [], []
    for h in range(height, tiers):
        rows = width + rank * (tiers - h - 1)
        plain.append(value[place : place + rows])
        place += rows
    while len(blocks) + 1 < tiers - height:
        blocks += unfold_two(value[place : place + rank + 2 * GRANULE])
        place += rank + 2 * GRANULE
    if len(blocks) < tiers - height:
        blocks.append(unfold_one(value[place : place + 3 * rank // 4]))
    return [
        jnp.concatenate([part[:width], block] + ([part[width:]] if part.shape[0] > width else []), axis=0)
        for part, block in zip(plain, blocks)
    ]


def join_pair(bit, s, t, width, rank, coeff_ref, next_ref):
    (pair,) = couple([(s[0], t[0])], width, rank)
    coeff_ref[...] = jnp.where(bit == 0, pair[0], pair[1])
    next_ref[...] = fold(merged(pair, s, t, width, rank), width, rank)


def pair_kernel(height, tiers, rank, width, own_ref, got_ref, passed_ref, coeff_ref, next_ref):
    core, _, bit = position(height)
    own, got, passed = own_ref[...], got_ref[...], passed_ref[...]
    far = jnp.concatenate([jnp.where(core == 0, got, passed), jnp.where(core == 0, passed, got)], axis=0)
    lower = jnp.where(bit == 0, own, far)
    upper = jnp.where(bit == 0, far, own)
    s, t = [unfold(value, height, tiers, rank, width) for value in (lower, upper)]
    join_pair(bit, s, t, width, rank, coeff_ref, next_ref)


def pair_level(kernel, height, tiers, rank, width, *sections):
    rows = folded_rows(height + 1, tiers, rank, width)
    return pl.pallas_call(
        functools.partial(kernel, height, tiers, rank, width),
        out_shape=[
            jax.ShapeDtypeStruct((width + rank * (tiers - height - 1), rank), F32),
            jax.ShapeDtypeStruct((rows, rank), F32),
        ],
        in_specs=vmem(len(sections)),
        out_specs=vmem(2),
        compiler_params=params(),
        name=f"level{height}",
    )(*sections)


def prepare_kernel(tiers, rank, width, solved_ref, images_ref, *refs):
    coeff_refs, out_ref = refs[:-1], refs[-1]
    last = tiers - 1
    found = [None] * last
    for h in reversed(range(last)):
        between = rank * (last - 1 - h)
        value = jnp.concatenate([coeff_refs[h][0:width, :], coeff_refs[h][width + between :, :]], axis=0)
        if between > 0:
            value = value - mm(jnp.concatenate(found[h + 1 :], axis=1), coeff_refs[h][width : width + between, :])
        found[h] = value
    images = images_ref[...]
    start = jnp.concatenate([solved_ref[...], images[:, rank * last :].T], axis=0)
    out_ref[...] = start - mm_nt(jnp.concatenate(found, axis=1), images[:, : rank * last])


def prepare(tiers, rank, width, solved, images, coeffs):
    rows = images.shape[0]
    return pl.pallas_call(
        functools.partial(prepare_kernel, tiers, rank, width),
        out_shape=jax.ShapeDtypeStruct((width + rank, rows), F32),
        in_specs=vmem(2 + len(coeffs)),
        out_specs=pl.BlockSpec(memory_space=pltpu.VMEM),
        compiler_params=params(),
        cost_estimate=pl.CostEstimate(
            flops=6 * (width + rank) * images.size, bytes_accessed=4 * images.size, transcendentals=0
        ),
        name="prepare",
    )(solved, images, *coeffs)


def finish_kernel(rank, width, own_ref, far_ref, ready_ref, out_ref):
    (own,), (far,) = [unfold(ref[...], 0, 1, rank, width) for ref in (own_ref, far_ref)]
    ((value, _),) = couple([(own, far)], width, rank)
    out_ref[...] = ready_ref[0:width, :] - mm(value, ready_ref[width:, :])


def finish(rank, width, own, far, ready):
    return pl.pallas_call(
        functools.partial(finish_kernel, rank, width),
        out_shape=jax.ShapeDtypeStruct((width, ready.shape[1]), F32),
        in_specs=vmem(3),
        out_specs=pl.BlockSpec(memory_space=pltpu.VMEM),
        compiler_params=params(),
        name="finish",
    )(own, far, ready)


def pack_kernel(bases_ref, given_ref, out_ref):
    tiers, rows, rank = bases_ref.shape
    width = given_ref.shape[0]
    for copy in range(CHIPS):
        for h in range(tiers):
            out_ref[copy, rows * h : rows * (h + 1), :] = bases_ref[h]
        for k in range(rows // rank):
            place = rows * tiers + width * k
            out_ref[copy, place : place + width, :] = given_ref[:, rank * k : rank * (k + 1)]


def pack(bases, given):
    tiers, rows, rank = bases.shape
    total = tiers * rows + given.size // rank
    return pl.pallas_call(
        pack_kernel,
        out_shape=jax.ShapeDtypeStruct((CHIPS, total, rank), bases.dtype),
        in_specs=vmem(2),
        out_specs=pl.BlockSpec(memory_space=pltpu.VMEM),
        compiler_params=params(),
        name="pack",
    )(bases, given)


def reorder_kernel(order_ref, inverse_ref, out_ref):
    columns = inverse_ref.shape[1]
    step = columns // MEMBERS
    inverse = inverse_ref[...]
    order = order_ref[...]
    for k in range(MEMBERS):
        given = lax.broadcasted_iota(jnp.int32, (step, columns), 0) + step * k
        chosen = jnp.where(given == order, 1.0, 0.0).astype(BF16)
        moved = lax.dot_general(inverse, chosen, (((1,), (1,)), ((), ())), preferred_element_type=F32)
        out_ref[:, step * k : step * (k + 1)] = moved.astype(BF16)


def reorder(order, inverse):
    return pl.pallas_call(
        reorder_kernel,
        out_shape=jax.ShapeDtypeStruct(inverse.shape, BF16),
        in_specs=vmem(2),
        out_specs=pl.BlockSpec(memory_space=pltpu.VMEM),
        compiler_params=params(),
        cost_estimate=pl.CostEstimate(
            flops=2 * inverse.size * inverse.shape[1], bytes_accessed=4 * inverse.size, transcendentals=0
        ),
        name="reorder",
    )(order, inverse)


def leaf_kernel(
    tiers, rank, width, inverse_ref, moved_ref, mine_ref, theirs_ref, own_ref, solved_ref, images_ref, keep_ref, give_ref, images_vmem, sem
):
    rows = inverse_ref.shape[0]
    core = lax.axis_index("rows") % CORES
    images, solved = None, None
    for chip in range(CHIPS):
        for ref, side in ((mine_ref, core), (theirs_ref, 1 - core)):
            columns = pl.ds(pl.multiple_of((CORES * chip + side) * rows, rows), rows)
            wide = jnp.concatenate([ref[chip, rows * h : rows * (h + 1)] for h in range(tiers)], axis=1)
            term = mm(inverse_ref[:, columns], wide, None)
            images = term if images is None else images + term
            given = ref[chip, rows * tiers :]
            given = jnp.concatenate([given[width * k : width * (k + 1)] for k in range(rows // rank)], axis=1)
            term = mm_nt(given, moved_ref[:, columns], None)
            solved = term if solved is None else solved + term
    solved_ref[...] = solved
    images_vmem[...] = images
    copy = pltpu.make_async_copy(images_vmem, images_ref, sem)
    copy.start()

    def pieces(value):
        high = value.astype(BF16)
        return high, (value - high.astype(F32)).astype(BF16)

    own = [own_ref[0, rows * h : rows * (h + 1)] for h in range(tiers)]
    flipped = jnp.concatenate(own, axis=1).T
    solved_high, solved_low = pieces(solved)
    few, each = width // MEMBERS, rank // MEMBERS

    def put(block, place, size):
        half = CHIPS * size
        first, second = block[:half], block[half:]
        for ref, value in (
            (keep_ref, jnp.where(core == 0, first, second)),
            (give_ref, jnp.where(core == 0, second, first)),
        ):
            if size % GRANULE == 0:
                ref[:, place : place + size, :] = value.reshape(CHIPS, size, rank)
                continue
            for chip in range(CHIPS):
                ref[chip, place : place + size, :] = value[size * chip : size * (chip + 1)]

    for h in range(tiers):
        top, middle, place = places(h, 0, tiers, rank)
        put(mm(solved_high, own[h], None) + mm(solved_low, own[h], None), top, few)
        high, low = pieces(images[:, rank * h : rank * (h + 1)])
        body = mm(flipped[rank * h :], high, None) + mm(flipped[rank * h :], low, None)
        for k in range(tiers - h - 1):
            put(body[rank * (k + 1) : rank * (k + 2)], place + each * k, each)
        if h % 2 == 0:
            even = body[:rank]
            continue
        odd = body[:rank]
        diagonal = jnp.where(mask_of(rank, jnp.equal), odd, 0.0).reshape(MEMBERS, each, rank)
        diagonal = jnp.broadcast_to(jnp.sum(diagonal, axis=1, keepdims=True), (MEMBERS, GRANULE, rank))
        put(diagonal.reshape(MEMBERS * GRANULE, rank), middle, GRANULE)
        put(jnp.where(mask_of(rank, jnp.greater_equal), even, odd), middle + GRANULE, each)
    copy.wait()


def leaf_step(tiers, rank, width, inverse, moved, mine, theirs, own):
    rows = inverse.shape[0]
    share = sum(pair_rows(h, tiers, rank) for h in range(0, tiers, 2))
    return pl.pallas_call(
        functools.partial(leaf_kernel, tiers, rank, width),
        out_shape=[
            jax.ShapeDtypeStruct((width, rows), F32),
            jax.ShapeDtypeStruct((rows, tiers * rank), F32),
            jax.ShapeDtypeStruct((CHIPS, share, rank), F32),
            jax.ShapeDtypeStruct((CHIPS, share, rank), F32),
        ],
        in_specs=vmem(5),
        out_specs=vmem(1) + [pl.BlockSpec(memory_space=pl.ANY)] + vmem(2),
        scratch_shapes=[pltpu.VMEM((rows, tiers * rank), F32), pltpu.SemaphoreType.DMA],
        compiler_params=params(),
        name="leaf",
    )(inverse, moved, mine, theirs, own)


def swap_cores(value):
    return lax.ppermute(value, "rows", [(i, i ^ 1) for i in range(MEMBERS)])


def swap_leaves(value, mask):
    return lax.ppermute(value, "leaf", [(i, i ^ mask) for i in range(lax.axis_size("leaf"))])


def groups_of(sets):
    return [
        [leaf * MEMBERS + chip * CORES + core for leaf in leaves for chip in range(CHIPS)]
        for leaves in sets
        for core in range(CORES)
    ]


def spread(value, sets):
    groups = groups_of(sets)
    count = len(groups[0])
    return lax.all_to_all(
        jnp.broadcast_to(value[None], (count,) + value.shape), BOTH, 0, 0, axis_index_groups=groups
    )


def local(right_side, point_order, leaf_inverse, bases):
    tiers, rank, width = bases.shape[1], bases.shape[2], right_side.shape[1]
    leaves = range(lax.axis_size("leaf"))
    rows = bases.shape[0]
    packed = pack(jnp.swapaxes(bases, 0, 1), right_side.T)
    groups = [[c + CORES * y for y in range(CHIPS)] for c in range(CORES)]
    mine = lax.all_to_all(packed, "rows", 0, 0, axis_index_groups=groups)
    theirs = swap_cores(mine)
    order, inverse, _ = lax.optimization_barrier((point_order, leaf_inverse, mine))
    moved = reorder(order, inverse)
    solved, images, keep, give = leaf_step(tiers, rank, width, leaf_inverse, moved, mine, theirs, packed)

    parts = keep + swap_cores(give)
    share = lax.all_to_all(parts, "rows", 0, 0, axis_index_groups=groups).sum(axis=0)

    cut = pair_rows(0, tiers, rank)
    tail = share[cut:]
    mine = spread(share[:cut], [tuple(range(i, i + 4)) for i in leaves if i % 4 == 0])
    theirs = swap_cores(mine)
    tail = tail + swap_leaves(tail, 1)
    tail = tail + swap_leaves(tail, 3)
    low, high, change = four_leaves(tiers, rank, width, mine, theirs)
    share = tail - change
    coeffs = [low, high]

    mine = spread(share, [(i, i ^ NEAR[2]) for i in leaves if not (i >> 2) & 1])
    theirs = swap_cores(mine)
    coeff, own = pair_level(first_pair_kernel, 2, tiers, rank, width, mine, theirs)
    coeffs.append(coeff)
    core = lax.axis_index("rows") % CORES
    for height in range(3, tiers - 1):
        half = own.shape[0] // CORES
        got = swap_leaves(lax.dynamic_slice_in_dim(own, core * half, half), NEAR[height])
        passed = swap_cores(got)
        coeff, own = pair_level(pair_kernel, height, tiers, rank, width, own, got, passed)
        coeffs.append(coeff)
    far = swap_leaves(own, NEAR[5])
    ready = prepare(tiers, rank, width, solved, images, coeffs)
    return finish(rank, width, own, far, ready).T


def solution(mesh):
    in_specs = (
        P(("leaf", "rows"), None),
        P("leaf", None),
        P(("leaf", "rows"), None),
        P(("leaf", "rows"), None, None),
    )
    out_specs = P(("leaf", "rows"), None)
    return jax.shard_map(local, mesh=mesh, in_specs=in_specs, out_specs=out_specs, check_vma=False)
```

```python
import functools

import jax
import jax.numpy as jnp
from jax import lax
from jax.experimental import pallas as pl
from jax.experimental.pallas import tpu as pltpu
from jax.sharding import PartitionSpec as P

F32 = jnp.float32
BF16 = jnp.bfloat16
FULL = lax.Precision.HIGHEST
TRIPLE = lax.Precision.HIGH
DOUBLINGS = 3
MEMBERS = 8
CORES = 2
CHIPS = MEMBERS // CORES
GRANULE = 8
VMEM_BYTES = 16 * 1024 * 1024
BOTH = ("leaf", "rows")
NEAR = {2: 4, 3: 8, 4: 16, 5: 48}


def mm(a, b, precision=TRIPLE):
    return lax.dot_general(a, b, (((1,), (0,)), ((), ())), precision=precision, preferred_element_type=F32)


def mm_nt(a, b, precision=TRIPLE):
    return lax.dot_general(a, b, (((1,), (1,)), ((), ())), precision=precision, preferred_element_type=F32)


def pair_rows(height, tiers, rank):
    return 2 * GRANULE + (rank // MEMBERS) * (2 * (tiers - height) - 2)


def places(height, first, tiers, rank):
    even = height - height % 2
    start = sum(pair_rows(h, tiers, rank) for h in range(first, even, 2))
    each = rank // MEMBERS
    skipped = each * (tiers - even - 1) if height % 2 else 0
    return start + (GRANULE // 2) * (height % 2), start + GRANULE, start + 2 * GRANULE + each + skipped


def solve(pairs, targets=None):
    rank = pairs[0][0].shape[0]
    eye = (
        lax.broadcasted_iota(jnp.int32, (rank, rank), 0) == lax.broadcasted_iota(jnp.int32, (rank, rank), 1)
    ).astype(F32)
    powers = [mm(left, right) for left, right in pairs]
    systems = [eye - power for power in powers]
    guesses = [eye + power for power in powers]
    for _ in range(DOUBLINGS):
        powers = [mm(power, power) for power in powers]
        guesses = [guess + mm(guess, power) for guess, power in zip(guesses, powers)]
    gaps = [eye - mm(system, guess) for system, guess in zip(systems, guesses)]
    size = functools.reduce(jnp.maximum, [jnp.sum(gap * gap) for gap in gaps])

    firsts = guesses if targets is None else [mm(target, guess) for target, guess in zip(targets, guesses)]

    def close():
        return [first + mm(first, gap) for first, gap in zip(firsts, gaps)]

    def refine(left, right, guess):
        system = eye - mm(left, right, FULL)
        entries = jnp.abs(system)
        bound = jnp.max(jnp.sum(entries, axis=0)) * jnp.max(jnp.sum(entries, axis=1))

        def measured(x):
            gap = eye - mm(system, x, FULL)
            return x, gap, jnp.sum(gap * gap)

        def step(carry):
            count, _, x, gap, size = carry
            return (count + 1, size) + measured(x + mm(x, gap, FULL))

        def more(carry):
            count, before, _, _, size = carry
            falls = jnp.logical_and(size > 1e-10, size < 0.5 * before)
            return jnp.logical_and(count < 80, jnp.logical_or(size >= 0.25, falls))

        first = measured(guess)
        first = lax.cond(first[2] < 0.25, lambda: first, lambda: measured(system.T / bound))
        return lax.while_loop(more, step, (0, jnp.float32(jnp.inf)) + first)[2]

    def far_off():
        found = [refine(left, right, guess) for (left, right), guess in zip(pairs, guesses)]
        if targets is None:
            return found
        return [mm(target, inverse, FULL) for target, inverse in zip(targets, found)]

    return lax.cond(size < 1e-6, close, far_off)


def position(height):
    leaf, row = lax.axis_index("leaf"), lax.axis_index("rows")
    core = row % CORES
    return core, core * CHIPS + row // CORES, (leaf // 2**height) % 2


def without(section, width, rank):
    if section.shape[0] == width + rank:
        return section[:width]
    return jnp.concatenate([section[:width], section[width + rank :]], axis=0)


def couple(children, width, rank):
    blocks = [(s[width : width + rank], t[width : width + rank]) for s, t in children]
    rests = [(without(s, width, rank), without(t, width, rank)) for s, t in children]
    targets = [t_r - mm(s_r, t_a) for (s_r, t_r), (_, t_a) in zip(rests, blocks)]
    found = solve(blocks, targets)
    return [(s_c, s_r - mm(s_c, s_a)) for s_c, (s_r, _), (s_a, _) in zip(found, rests, blocks)]


def couple_wide(children, width, rank):
    blocks = [(s[width : width + rank], t[width : width + rank]) for s, t in children]
    found = []
    for (s, t), (s_a, t_a), inverse in zip(children, blocks, solve(blocks)):
        flipped = inverse.T
        upper = jnp.concatenate([-mm(t_a, inverse), flipped], axis=1)
        lower = jnp.concatenate([inverse, -mm(s_a, flipped)], axis=1)
        rests = jnp.concatenate([without(s, width, rank), without(t, width, rank)], axis=1)
        both = mm(rests, jnp.concatenate([upper, lower], axis=0))
        found.append((both[:, :rank], both[:, rank:]))
    return found


def images_of(s, t, width, rank):
    return jnp.concatenate([s[width + rank :], t[width + rank :]], axis=1)


def gathered(halves, node, height, first, tiers, rank, width):
    each, few = rank // MEMBERS, width // MEMBERS
    chips = range(CHIPS * node, CHIPS * (node + 1))

    def joined(start):
        rows = slice(start, start + each)
        return [half[chips.start : chips.stop, rows, :].reshape(CHIPS * each, rank) for half in halves]

    _, middle, _ = places(height, first, tiers, rank)
    block = jnp.concatenate(joined(middle + GRANULE), axis=0)
    diagonal = sum(half[chip, middle : middle + 1, :] for half in halves for chip in chips)
    blocks = unfold_two(jnp.concatenate([block, diagonal], axis=0))
    sections = []
    for h in (height, height + 1):
        top, _, place = places(h, first, tiers, rank)
        parts = [half[chip, top : top + few, :] for half in halves for chip in chips] + [blocks[h - height]]
        for k in range(tiers - h - 1):
            parts += joined(place + each * k)
        sections.append(jnp.concatenate(parts, axis=0))
    return sections


def by_core(core, mine_ref, theirs_ref, body):
    @pl.when(core == 0)
    def _():
        body((mine_ref, theirs_ref))

    @pl.when(core != 0)
    def _():
        body((theirs_ref, mine_ref))


def vmem(count):
    return [pl.BlockSpec(memory_space=pltpu.VMEM)] * count


def params():
    return pltpu.CompilerParams(vmem_limit_bytes=VMEM_BYTES)


def own_rows(both, member, wide_ref, rank):
    each = rank // MEMBERS
    wide_ref[...] = both
    slices = [
        wide_ref[pl.ds(pl.multiple_of(rank * k + member * each, each), each), :] for k in range(both.shape[0] // rank)
    ]
    return jnp.concatenate(slices, axis=0)


def four_leaves_kernel(
    tiers, rank, width, mine_ref, theirs_ref, low_ref, high_ref, change_ref, wide_a, wide_b, wide_c, top_ref
):
    by_core(
        position(0)[0],
        mine_ref,
        theirs_ref,
        functools.partial(
            join_four, tiers, rank, width, low_ref, high_ref, change_ref, (wide_a, wide_b, wide_c), top_ref
        ),
    )


def join_four(tiers, rank, width, low_ref, high_ref, change_ref, wide_refs, top_ref, halves):
    _, member, odd = position(0)
    upper = position(1)[2]
    each, few = rank // MEMBERS, width // MEMBERS
    nodes = [gathered(halves, k, 0, 0, tiers, rank, width) for k in range(4)]
    tops, blocks = [None] * tiers, [None] * tiers

    def note(both, images, first, wide_ref):
        top = mm_nt(both[:width], images[rank * (2 - first) :])
        rows = own_rows(both[width:], member, wide_ref, rank)
        for h in range(2, tiers):
            g = h - first
            term = mm_nt(rows[each * g :], images[rank * g : rank * (g + 1)])
            part = top[:, rank * (h - 2) : rank * (h - 1)]
            blocks[h] = term if blocks[h] is None else blocks[h] + term
            tops[h] = part if tops[h] is None else tops[h] + part

    pairs = [(nodes[0], nodes[1]), (nodes[2], nodes[3])]
    found = couple_wide([(s[0], t[0]) for s, t in pairs], width, rank)
    picked = [jnp.where(odd == 0, s_c, t_c) for s_c, t_c in found]
    low_ref[...] = jnp.where(upper == 0, picked[0], picked[1])
    joined = []
    for (s_c, t_c), (s, t), wide_ref in zip(found, pairs, wide_refs):
        both = jnp.concatenate([s_c, t_c], axis=1)
        images = images_of(s[0], t[0], width, rank)
        joined.append(s[1] + t[1] - mm_nt(both, images[:rank]))
        note(both, images, 1, wide_ref)
    ((s_c, t_c),) = couple_wide([tuple(joined)], width, rank)
    high_ref[...] = jnp.where(upper == 0, s_c, t_c)
    note(jnp.concatenate([s_c, t_c], axis=1), images_of(*joined, width, rank), 2, wide_refs[2])
    for h in range(2, tiers):
        _, _, place = places(h, 2, tiers, rank)
        if h + 1 < tiers:
            change_ref[place : place + each * (tiers - h - 1), :] = blocks[h][each:]
        for k in range(MEMBERS):
            top_ref[k, few * (h - 2) : few * (h - 1), :] = tops[h][few * k : few * (k + 1)]
    mine = top_ref[member]
    row = lax.broadcasted_iota(jnp.int32, (each, rank), 0) + member * each
    column = lax.broadcasted_iota(jnp.int32, (each, rank), 1)
    for h in range(2, tiers, 2):
        top, middle, _ = places(h, 2, tiers, rank)
        change_ref[top : top + GRANULE, :] = mine[few * (h - 2) : few * h]
        a, b = blocks[h][:each], blocks[h + 1][:each]
        diagonal = jnp.sum(jnp.where(row == column, b, 0.0), axis=0, keepdims=True)
        change_ref[middle : middle + GRANULE, :] = jnp.broadcast_to(diagonal, (GRANULE, rank))
        change_ref[middle + GRANULE : middle + GRANULE + each, :] = jnp.where(row >= column, a, b)


def four_leaves(tiers, rank, width, mine, theirs):
    rows = sum(pair_rows(h, tiers, rank) for h in range(2, tiers, 2))
    return pl.pallas_call(
        functools.partial(four_leaves_kernel, tiers, rank, width),
        out_shape=[
            jax.ShapeDtypeStruct((width + rank * (tiers - 1), rank), F32),
            jax.ShapeDtypeStruct((width + rank * (tiers - 2), rank), F32),
            jax.ShapeDtypeStruct((rows, rank), F32),
        ],
        in_specs=vmem(2),
        out_specs=vmem(3),
        scratch_shapes=[pltpu.VMEM((rank * (tiers - k), 2 * rank), F32) for k in (1, 1, 2)]
        + [pltpu.VMEM((MEMBERS, (width // MEMBERS) * (tiers - 2), rank), F32)],
        compiler_params=params(),
        name="level0",
    )(mine, theirs)


def merged(coeffs, s, t, width, rank):
    both = jnp.concatenate(coeffs, axis=1)
    images = images_of(s[0], t[0], width, rank)
    top = mm_nt(both[:width], images)
    out = []
    for g in range(len(s) - 1):
        columns = slice(rank * g, rank * (g + 1))
        low = mm_nt(both[width + rank * g :], images[columns])
        out.append(s[g + 1] + t[g + 1] - jnp.concatenate([top[:, columns], low], axis=0))
    return out


def first_pair_kernel(height, tiers, rank, width, mine_ref, theirs_ref, coeff_ref, next_ref):
    core, _, bit = position(height)

    def body(halves):
        nodes = [
            sum([gathered(halves, k, h, height, tiers, rank, width) for h in range(height, tiers, 2)], []) for k in range(2)
        ]
        join_pair(bit, nodes[0], nodes[1], width, rank, coeff_ref, next_ref)

    by_core(core, mine_ref, theirs_ref, body)


def mask_of(rank, compare):
    return compare(
        lax.broadcasted_iota(jnp.int32, (rank, rank), 0), lax.broadcasted_iota(jnp.int32, (rank, rank), 1)
    )


def fold_two(a, b):
    rank = a.shape[0]
    diagonal = jnp.sum(jnp.where(mask_of(rank, jnp.equal), b, 0.0), axis=0, keepdims=True)
    return jnp.concatenate(
        [jnp.where(mask_of(rank, jnp.greater_equal), a, b), jnp.broadcast_to(diagonal, (2 * GRANULE, rank))], axis=0
    )


def unfold_two(folded):
    rank = folded.shape[1]
    block = folded[:rank]
    flipped = block.T
    a = jnp.where(mask_of(rank, jnp.greater_equal), block, flipped)
    b = jnp.where(mask_of(rank, jnp.less), block, flipped)
    diagonal = jnp.broadcast_to(folded[rank : rank + 1], (rank, rank))
    return a, jnp.where(mask_of(rank, jnp.equal), diagonal, b)


def fold_one(a):
    half, part = a.shape[0] // 2, a.shape[0] // 4
    corner = a[half:, half:]
    return jnp.concatenate([a[:half], jnp.concatenate([corner[:part], corner[part:]], axis=1)], axis=0)


def unfold_one(folded):
    half = folded.shape[1] // 2
    upper, corner = folded[:half], folded[half:]
    corner = jnp.concatenate([corner[:, :half], corner[:, half:]], axis=0)
    return jnp.concatenate([upper, jnp.concatenate([upper.T[half:], corner], axis=1)], axis=0)


def folded_rows(height, tiers, rank, width):
    count = tiers - height
    pairs, single = count // 2, count % 2
    plain = sum(width + rank * (k - 1) for k in range(1, count + 1))
    return plain + pairs * (rank + 2 * GRANULE) + single * (3 * rank // 4)


def fold(sections, width, rank):
    parts = [without(section, width, rank) for section in sections]
    blocks = [section[width : width + rank] for section in sections]
    while len(blocks) > 1:
        parts.append(fold_two(blocks[0], blocks[1]))
        blocks = blocks[2:]
    parts += [fold_one(block) for block in blocks]
    return jnp.concatenate(parts, axis=0)


def unfold(value, height, tiers, rank, width):
    place, plain, blocks = 0, [], []
    for h in range(height, tiers):
        rows = width + rank * (tiers - h - 1)
        plain.append(value[place : place + rows])
        place += rows
    while len(blocks) + 1 < tiers - height:
        blocks += unfold_two(value[place : place + rank + 2 * GRANULE])
        place += rank + 2 * GRANULE
    if len(blocks) < tiers - height:
        blocks.append(unfold_one(value[place : place + 3 * rank // 4]))
    return [
        jnp.concatenate([part[:width], block] + ([part[width:]] if part.shape[0] > width else []), axis=0)
        for part, block in zip(plain, blocks)
    ]


def join_pair(bit, s, t, width, rank, coeff_ref, next_ref):
    (pair,) = couple([(s[0], t[0])], width, rank)
    coeff_ref[...] = jnp.where(bit == 0, pair[0], pair[1])
    next_ref[...] = fold(merged(pair, s, t, width, rank), width, rank)


def pair_kernel(height, tiers, rank, width, own_ref, got_ref, passed_ref, coeff_ref, next_ref):
    core, _, bit = position(height)
    own, got, passed = own_ref[...], got_ref[...], passed_ref[...]
    far = jnp.concatenate([jnp.where(core == 0, got, passed), jnp.where(core == 0, passed, got)], axis=0)
    lower = jnp.where(bit == 0, own, far)
    upper = jnp.where(bit == 0, far, own)
    s, t = [unfold(value, height, tiers, rank, width) for value in (lower, upper)]
    join_pair(bit, s, t, width, rank, coeff_ref, next_ref)


def pair_level(kernel, height, tiers, rank, width, *sections):
    rows = folded_rows(height + 1, tiers, rank, width)
    return pl.pallas_call(
        functools.partial(kernel, height, tiers, rank, width),
        out_shape=[
            jax.ShapeDtypeStruct((width + rank * (tiers - height - 1), rank), F32),
            jax.ShapeDtypeStruct((rows, rank), F32),
        ],
        in_specs=vmem(len(sections)),
        out_specs=vmem(2),
        compiler_params=params(),
        name=f"level{height}",
    )(*sections)


def prepare_kernel(tiers, rank, width, solved_ref, images_ref, *refs):
    coeff_refs, out_ref = refs[:-1], refs[-1]
    last = tiers - 1
    found = [None] * last
    for h in reversed(range(last)):
        between = rank * (last - 1 - h)
        value = jnp.concatenate([coeff_refs[h][0:width, :], coeff_refs[h][width + between :, :]], axis=0)
        if between > 0:
            value = value - mm(jnp.concatenate(found[h + 1 :], axis=1), coeff_refs[h][width : width + between, :])
        found[h] = value
    images = images_ref[...]
    start = jnp.concatenate([solved_ref[...], images[:, rank * last :].T], axis=0)
    out_ref[...] = start - mm_nt(jnp.concatenate(found, axis=1), images[:, : rank * last])


def prepare(tiers, rank, width, solved, images, coeffs):
    rows = images.shape[0]
    return pl.pallas_call(
        functools.partial(prepare_kernel, tiers, rank, width),
        out_shape=jax.ShapeDtypeStruct((width + rank, rows), F32),
        in_specs=vmem(2 + len(coeffs)),
        out_specs=pl.BlockSpec(memory_space=pltpu.VMEM),
        compiler_params=params(),
        cost_estimate=pl.CostEstimate(
            flops=6 * (width + rank) * images.size, bytes_accessed=4 * images.size, transcendentals=0
        ),
        name="prepare",
    )(solved, images, *coeffs)


def finish_kernel(rank, width, own_ref, far_ref, ready_ref, out_ref):
    (own,), (far,) = [unfold(ref[...], 0, 1, rank, width) for ref in (own_ref, far_ref)]
    ((value, _),) = couple([(own, far)], width, rank)
    out_ref[...] = ready_ref[0:width, :] - mm(value, ready_ref[width:, :])


def finish(rank, width, own, far, ready):
    return pl.pallas_call(
        functools.partial(finish_kernel, rank, width),
        out_shape=jax.ShapeDtypeStruct((width, ready.shape[1]), F32),
        in_specs=vmem(3),
        out_specs=pl.BlockSpec(memory_space=pltpu.VMEM),
        compiler_params=params(),
        name="finish",
    )(own, far, ready)


def pack_kernel(bases_ref, given_ref, out_ref):
    tiers, rows, rank = bases_ref.shape
    width = given_ref.shape[0]
    for copy in range(CHIPS):
        for h in range(tiers):
            out_ref[copy, rows * h : rows * (h + 1), :] = bases_ref[h]
        for k in range(rows // rank):
            place = rows * tiers + width * k
            out_ref[copy, place : place + width, :] = given_ref[:, rank * k : rank * (k + 1)]


def pack(bases, given):
    tiers, rows, rank = bases.shape
    total = tiers * rows + given.size // rank
    return pl.pallas_call(
        pack_kernel,
        out_shape=jax.ShapeDtypeStruct((CHIPS, total, rank), bases.dtype),
        in_specs=vmem(2),
        out_specs=pl.BlockSpec(memory_space=pltpu.VMEM),
        compiler_params=params(),
        name="pack",
    )(bases, given)


def reorder_kernel(order_ref, inverse_ref, out_ref):
    columns = inverse_ref.shape[1]
    step = columns // MEMBERS
    inverse = inverse_ref[...]
    order = order_ref[...]
    for k in range(MEMBERS):
        given = lax.broadcasted_iota(jnp.int32, (step, columns), 0) + step * k
        chosen = jnp.where(given == order, 1.0, 0.0).astype(BF16)
        moved = lax.dot_general(inverse, chosen, (((1,), (1,)), ((), ())), preferred_element_type=F32)
        out_ref[:, step * k : step * (k + 1)] = moved.astype(BF16)


def reorder(order, inverse):
    return pl.pallas_call(
        reorder_kernel,
        out_shape=jax.ShapeDtypeStruct(inverse.shape, BF16),
        in_specs=vmem(2),
        out_specs=pl.BlockSpec(memory_space=pltpu.VMEM),
        compiler_params=params(),
        cost_estimate=pl.CostEstimate(
            flops=2 * inverse.size * inverse.shape[1], bytes_accessed=4 * inverse.size, transcendentals=0
        ),
        name="reorder",
    )(order, inverse)


def leaf_kernel(
    tiers, rank, width, inverse_ref, moved_ref, mine_ref, theirs_ref, own_ref, solved_ref, images_ref, keep_ref, give_ref, images_vmem, sem
):
    rows = inverse_ref.shape[0]
    core = lax.axis_index("rows") % CORES
    images, solved = None, None
    for chip in range(CHIPS):
        for ref, side in ((mine_ref, core), (theirs_ref, 1 - core)):
            columns = pl.ds(pl.multiple_of((CORES * chip + side) * rows, rows), rows)
            wide = jnp.concatenate([ref[chip, rows * h : rows * (h + 1)] for h in range(tiers)], axis=1)
            term = mm(inverse_ref[:, columns], wide, None)
            images = term if images is None else images + term
            given = ref[chip, rows * tiers :]
            given = jnp.concatenate([given[width * k : width * (k + 1)] for k in range(rows // rank)], axis=1)
            term = mm_nt(given, moved_ref[:, columns], None)
            solved = term if solved is None else solved + term
    solved_ref[...] = solved
    images_vmem[...] = images
    copy = pltpu.make_async_copy(images_vmem, images_ref, sem)
    copy.start()

    def pieces(value):
        high = value.astype(BF16)
        return high, (value - high.astype(F32)).astype(BF16)

    own = [own_ref[0, rows * h : rows * (h + 1)] for h in range(tiers)]
    flipped = jnp.concatenate(own, axis=1).T
    solved_high, solved_low = pieces(solved)
    few, each = width // MEMBERS, rank // MEMBERS

    def put(block, place, size):
        half = CHIPS * size
        first, second = block[:half], block[half:]
        for ref, value in (
            (keep_ref, jnp.where(core == 0, first, second)),
            (give_ref, jnp.where(core == 0, second, first)),
        ):
            if size % GRANULE == 0:
                ref[:, place : place + size, :] = value.reshape(CHIPS, size, rank)
                continue
            for chip in range(CHIPS):
                ref[chip, place : place + size, :] = value[size * chip : size * (chip + 1)]

    for h in range(tiers):
        top, middle, place = places(h, 0, tiers, rank)
        put(mm(solved_high, own[h], None) + mm(solved_low, own[h], None), top, few)
        high, low = pieces(images[:, rank * h : rank * (h + 1)])
        body = mm(flipped[rank * h :], high, None) + mm(flipped[rank * h :], low, None)
        for k in range(tiers - h - 1):
            put(body[rank * (k + 1) : rank * (k + 2)], place + each * k, each)
        if h % 2 == 0:
            even = body[:rank]
            continue
        odd = body[:rank]
        diagonal = jnp.where(mask_of(rank, jnp.equal), odd, 0.0).reshape(MEMBERS, each, rank)
        diagonal = jnp.broadcast_to(jnp.sum(diagonal, axis=1, keepdims=True), (MEMBERS, GRANULE, rank))
        put(diagonal.reshape(MEMBERS * GRANULE, rank), middle, GRANULE)
        put(jnp.where(mask_of(rank, jnp.greater_equal), even, odd), middle + GRANULE, each)
    copy.wait()


def leaf_step(tiers, rank, width, inverse, moved, mine, theirs, own):
    rows = inverse.shape[0]
    share = sum(pair_rows(h, tiers, rank) for h in range(0, tiers, 2))
    return pl.pallas_call(
        functools.partial(leaf_kernel, tiers, rank, width),
        out_shape=[
            jax.ShapeDtypeStruct((width, rows), F32),
            jax.ShapeDtypeStruct((rows, tiers * rank), F32),
            jax.ShapeDtypeStruct((CHIPS, share, rank), F32),
            jax.ShapeDtypeStruct((CHIPS, share, rank), F32),
        ],
        in_specs=vmem(5),
        out_specs=vmem(1) + [pl.BlockSpec(memory_space=pl.ANY)] + vmem(2),
        scratch_shapes=[pltpu.VMEM((rows, tiers * rank), F32), pltpu.SemaphoreType.DMA],
        compiler_params=params(),
        name="leaf",
    )(inverse, moved, mine, theirs, own)


def swap_cores(value):
    return lax.ppermute(value, "rows", [(i, i ^ 1) for i in range(MEMBERS)])


def swap_leaves(value, mask):
    return lax.ppermute(value, "leaf", [(i, i ^ mask) for i in range(lax.axis_size("leaf"))])


def groups_of(sets):
    return [
        [leaf * MEMBERS + chip * CORES + core for leaf in leaves for chip in range(CHIPS)]
        for leaves in sets
        for core in range(CORES)
    ]


def spread(value, sets):
    groups = groups_of(sets)
    count = len(groups[0])
    return lax.all_to_all(
        jnp.broadcast_to(value[None], (count,) + value.shape), BOTH, 0, 0, axis_index_groups=groups
    )


def local(right_side, point_order, leaf_inverse, bases):
    tiers, rank, width = bases.shape[1], bases.shape[2], right_side.shape[1]
    leaves = range(lax.axis_size("leaf"))
    rows = bases.shape[0]
    packed = pack(jnp.swapaxes(bases, 0, 1), right_side.T)
    groups = [[c + CORES * y for y in range(CHIPS)] for c in range(CORES)]
    mine = lax.all_to_all(packed, "rows", 0, 0, axis_index_groups=groups)
    theirs = swap_cores(mine)
    order, inverse, _ = lax.optimization_barrier((point_order, leaf_inverse, mine))
    moved = reorder(order, inverse)
    solved, images, keep, give = leaf_step(tiers, rank, width, leaf_inverse, moved, mine, theirs, packed)

    parts = keep + swap_cores(give)
    share = lax.all_to_all(parts, "rows", 0, 0, axis_index_groups=groups).sum(axis=0)

    cut = pair_rows(0, tiers, rank)
    tail = share[cut:]
    mine = spread(share[:cut], [tuple(range(i, i + 4)) for i in leaves if i % 4 == 0])
    theirs = swap_cores(mine)
    tail = tail + swap_leaves(tail, 1)
    tail = tail + swap_leaves(tail, 3)
    low, high, change = four_leaves(tiers, rank, width, mine, theirs)
    share = tail - change
    coeffs = [low, high]

    mine = spread(share, [(i, i ^ NEAR[2]) for i in leaves if not (i >> 2) & 1])
    theirs = swap_cores(mine)
    coeff, own = pair_level(first_pair_kernel, 2, tiers, rank, width, mine, theirs)
    coeffs.append(coeff)
    core = lax.axis_index("rows") % CORES
    for height in range(3, tiers - 1):
        half = own.shape[0] // CORES
        got = swap_leaves(lax.dynamic_slice_in_dim(own, core * half, half), NEAR[height])
        passed = swap_cores(got)
        coeff, own = pair_level(pair_kernel, height, tiers, rank, width, own, got, passed)
        coeffs.append(coeff)
    far = swap_leaves(own, NEAR[5])
    ready = prepare(tiers, rank, width, solved, images, coeffs)
    return finish(rank, width, own, far, ready).T


def solution(mesh):
    in_specs = (
        P(("leaf", "rows"), None),
        P("leaf", None),
        P(("leaf", "rows"), None),
        P(("leaf", "rows"), None, None),
    )
    out_specs = P(("leaf", "rows"), None)
    return jax.shard_map(local, mesh=mesh, in_specs=in_specs, out_specs=out_specs, check_vma=False)
```
